32 devices in a mesh: group: 2 (over y), tenant: 16 (over z, x, core).
Axes of the slice: x: 2, y: 2, z: 4, core: 2. Of those that a mesh axis runs over, the one named last changes fastest.
Arguments:
- tokens: bfloat16 [4096, 8192], P(('group', 'tenant')), parts along dimension 0, may hold values from -6 to 6
- grad_up: bfloat16 [4096, 16384], P(('group', 'tenant')), parts along dimension 0, may hold values from -6 to 6
- tenant_ids: int32 [4096], P(('group', 'tenant')), parts along dimension 0, may hold values from 0 to 1, as said below
- expert_ids: int32 [4096, 2], P(('group', 'tenant')), parts along dimension 0, may hold values from 0 to 7, as said below
- adapter_down: bfloat16 [16, 16, 8192], P('tenant'), may hold values from -0.0625 to 0.0625
- adapter_up: bfloat16 [16, 16, 16384], P('tenant'), may hold values from -0.046875 to 0.046875
- router: bfloat16 [16, 8192], replicated, may hold values from -0.0625 to 0.0625
Outputs:
- token_grad: bfloat16 [4096, 8192], P(('group', 'tenant')), parts along dimension 0
- grad_down: float32 [32, 16, 8192], P(('group', 'tenant')), parts along dimension 0
- grad_upper: float32 [32, 16, 16384], P(('group', 'tenant')), parts along dimension 0
- router_grad: float32 [32, 8192], P(('group', 'tenant')), parts along dimension 0
The draws below stay inside these ranges and needn't reach their ends.
There are 2 independent parts, one for each index of `group`. The reference program is written for one: setup_inputs(seed, part) draws one part's arguments, and reference() takes and returns one part's arrays. A program takes and returns all parts, laid end to end along the dimension named above; an argument that names none is the same for every part. Nothing has to cross between parts.
Inputs may be any that keep to these rules, and one draw needn't show every extreme that they name: `tenant_ids`: the 128 tokens of one index of tenant form 2 blocks of equal length, one for each tenant, in an order drawn for each index. `expert_ids`: id j of tenant t names expert 8 * t + j, whose factors device 8 * t + j along the mesh axis `tenant` holds. A token's two ids differ. Among the tokens of one index of tenant, every expert is named by exactly 16.
All inputs are finite; a program needn't handle non-finite values.
Results may differ from the reference program's by a relative error of at most 0.0062.
Values may be sent and summed in bfloat16 or wider, within the bound.
A program may use at most 128 MiB of HBM per device.

```python
import jax
import jax.numpy as jnp
from jax import lax

D = 8192
FFW = 16384
RANK = 16
EXP_TEN = 8
TOK_DEV = 128
TOKENS = 2048
EXPERTS = 16
TENANTS = 2
CAP = 16
N_TENANT = 16


def route_table(key):
    blocks = TOKENS // TOK_DEV
    per_tenant = TOK_DEV // TENANTS
    key_order, key_cycle, key_flip = jax.random.split(key, 3)
    order_scores = jax.random.randint(key_order, (blocks, TENANTS), 0, 1 << 20) * TENANTS + jnp.arange(TENANTS, dtype=jnp.int32)
    orders = jnp.argsort(order_scores, axis=1).astype(jnp.int32)
    position = jnp.arange(TOK_DEV, dtype=jnp.int32)
    block_of = position // per_tenant
    local_index = position % per_tenant
    tenant = jnp.take_along_axis(orders, jnp.broadcast_to(block_of[None, :], (blocks, TOK_DEV)), axis=1)
    scores = jax.random.randint(key_cycle, (blocks, TENANTS, EXP_TEN), 0, 1 << 20) * EXP_TEN + jnp.arange(EXP_TEN, dtype=jnp.int32)
    cycles = jnp.argsort(scores, axis=2).astype(jnp.int32)
    token_cycle = jnp.take_along_axis(cycles, jnp.broadcast_to(block_of[None, :, None], (blocks, TOK_DEV, 1)), axis=1)
    first_slot = jnp.broadcast_to((2 * local_index % EXP_TEN)[None, :, None], (blocks, TOK_DEV, 1))
    second_slot = jnp.broadcast_to(((2 * local_index + 1) % EXP_TEN)[None, :, None], (blocks, TOK_DEV, 1))
    first_expert = jnp.take_along_axis(token_cycle, first_slot, axis=2)[:, :, 0]
    second_expert = jnp.take_along_axis(token_cycle, second_slot, axis=2)[:, :, 0]
    flip = jax.random.randint(key_flip, (blocks, TOK_DEV), 0, 2)
    straight = jnp.stack([first_expert, second_expert], axis=2)
    swapped = jnp.stack([second_expert, first_expert], axis=2)
    paired_ids = jnp.where(flip[:, :, None] == 1, swapped, straight)
    return (tenant.reshape(TOKENS).astype(jnp.int32), paired_ids.reshape(TOKENS, 2).astype(jnp.int32))


def draw_tenant_ids(key, part):
    tenant, paired_ids = route_table(key)
    return tenant


def draw_expert_ids(key, part):
    tenant, paired_ids = route_table(key)
    return paired_ids


def levels(own_key, extent, pieces, smallest, largest):
    def one(axis_at, parts):
        steps = jax.random.uniform(jax.random.fold_in(jax.random.fold_in(own_key, 6), axis_at), (parts,), jnp.float32, smallest / len(pieces), largest / len(pieces))
        return jnp.repeat(jnp.exp(steps), extent[axis_at] // parts).reshape((-1,) + (1,) * (len(extent) - axis_at - 1))

    gain = one(*pieces[0])
    for cut in pieces[1:]:
        gain = gain * one(*cut)
    return gain


def noise(key, extent, scale, most, pieces=(), kind=jnp.bfloat16):
    level = levels(key, extent, pieces, -0.22, 0.18) if pieces else 1.0
    drawn = jax.random.normal(key, extent, jnp.float32) * scale * level
    return jnp.minimum(jnp.maximum(drawn, -most), most).astype(kind)


def setup_inputs(seed: int = 0, part: int = 0) -> dict:
    keys = jax.random.split(jax.random.key(seed), 8)
    part_keys = jax.random.split(jax.random.fold_in(keys[7], part), 8)
    tokens = noise(part_keys[0], (TOKENS, D), 1.0, 6.0, ((0, 16),))
    grad_up = noise(part_keys[1], (TOKENS, FFW), 1.0, 6.0, ((0, 16),))
    tenant_ids = draw_tenant_ids(jax.random.fold_in(jax.random.fold_in(keys[7], part), 71), part)
    expert_ids = draw_expert_ids(jax.random.fold_in(jax.random.fold_in(keys[7], part), 71), part)
    adapter_down = noise(keys[4], (EXPERTS, RANK, D), D ** -0.5, 0.0625, ((0, 16),))
    adapter_up = noise(keys[5], (EXPERTS, RANK, FFW), FFW ** -0.5, 0.046875, ((0, 16),))
    router = noise(keys[6], (EXPERTS, D), D ** -0.5, 0.0625)
    return dict(tokens=tokens, grad_up=grad_up, tenant_ids=tenant_ids, expert_ids=expert_ids, adapter_down=adapter_down, adapter_up=adapter_up, router=router)


adapter_scale_factor = 2.0


def reference(tokens, grad_up, tenant_ids, expert_ids, adapter_down, adapter_up, router):
    global_ids = (tenant_ids[:, None] * EXP_TEN + expert_ids).astype(jnp.int32)
    logits = lax.dot_general(tokens, router, (((1,), (1,)), ((), ())), preferred_element_type=jnp.float32)
    picked = jnp.take_along_axis(logits, global_ids, axis=1)
    first_gate = jax.nn.sigmoid(picked[:, 0] - picked[:, 1])
    gate_pair = jnp.stack([first_gate, 1.0 - first_gate], axis=1)
    gate_sent = gate_pair.astype(jnp.bfloat16)
    flat_ids = global_ids.reshape(-1)
    slot_total = flat_ids.shape[0]
    slot_order = jnp.argsort(flat_ids, stable=True).astype(jnp.int32)
    counts = jnp.zeros((EXPERTS,), jnp.int32).at[flat_ids].add(1)
    starts = (jnp.cumsum(counts) - counts).astype(jnp.int32)
    most_rows = N_TENANT * CAP
    flat_gates = gate_sent.reshape(-1)

    def per_expert(running, expert):
        grad_tokens, gate_grads = running
        offsets = jnp.arange(most_rows, dtype=jnp.int32)
        live_mask = offsets < counts[expert]
        place = jnp.clip(starts[expert] + offsets, 0, slot_total - 1).astype(jnp.int32)
        slot_index = slot_order[place]
        token_index = (slot_index // 2).astype(jnp.int32)
        keep = live_mask[:, None]
        rows_in = jnp.where(keep, tokens[token_index], jnp.zeros((), jnp.bfloat16))
        grads_in = jnp.where(keep, grad_up[token_index], jnp.zeros((), jnp.bfloat16))
        incoming_gate_values = jnp.where(live_mask, flat_gates[slot_index], jnp.zeros((), jnp.bfloat16)).astype(jnp.float32)
        down = adapter_down[expert]
        upper = adapter_up[expert]
        reduced_rank_activations = lax.dot_general(rows_in, down, (((1,), (1,)), ((), ())), preferred_element_type=jnp.float32)
        returned_rank_gradient = lax.dot_general(grads_in, upper, (((1,), (1,)), ((), ())), preferred_element_type=jnp.float32)
        position_gate_value = (adapter_scale_factor * jnp.sum(reduced_rank_activations * returned_rank_gradient, axis=1)).astype(jnp.bfloat16)
        gate_weighted_output = (adapter_scale_factor * incoming_gate_values[:, None] * returned_rank_gradient).astype(jnp.bfloat16)
        scaled_reduced_activations = (adapter_scale_factor * incoming_gate_values[:, None] * reduced_rank_activations).astype(jnp.bfloat16)
        slot_rows = jnp.dot(gate_weighted_output, down, preferred_element_type=jnp.float32).astype(jnp.bfloat16)
        down_grad = lax.dot_general(gate_weighted_output, rows_in, (((0,), (0,)), ((), ())), preferred_element_type=jnp.float32)
        upper_grad = lax.dot_general(scaled_reduced_activations, grads_in, (((0,), (0,)), ((), ())), preferred_element_type=jnp.float32)
        grad_tokens = grad_tokens.at[token_index].add(jnp.where(keep, slot_rows.astype(jnp.float32), jnp.zeros((), jnp.float32)))
        gate_grads = gate_grads.at[slot_index].add(jnp.where(live_mask, position_gate_value.astype(jnp.float32), jnp.zeros((), jnp.float32)))
        return (grad_tokens, gate_grads), (down_grad, upper_grad)

    initial = (jnp.zeros((TOKENS, D), jnp.float32), jnp.zeros((slot_total,), jnp.float32))
    (expert_grad, gate_grads), (grad_down, grad_upper) = lax.scan(per_expert, initial, jnp.arange(EXPERTS, dtype=jnp.int32))
    gate_grads = gate_grads.reshape(TOKENS, 2)
    logit_grad = first_gate * (1.0 - first_gate) * (gate_grads[:, 0] - gate_grads[:, 1])
    logit_sent = logit_grad.astype(jnp.bfloat16)
    columns = jnp.arange(EXPERTS, dtype=jnp.int32)[None, :]
    nothing = jnp.zeros((), jnp.bfloat16)
    signed = jnp.where(columns == global_ids[:, 0:1], logit_sent[:, None], nothing) - jnp.where(columns == global_ids[:, 1:2], logit_sent[:, None], nothing)
    router_grad = lax.dot_general(signed, tokens, (((0,), (0,)), ((), ())), preferred_element_type=jnp.float32)
    router_term = jnp.dot(signed, router, preferred_element_type=jnp.float32)
    token_grad = (expert_grad + router_term).astype(jnp.bfloat16)
    return token_grad, grad_down, grad_upper, router_grad
```

```python
import jax
import jax.numpy as jnp
from jax import lax
from jax.sharding import PartitionSpec as P

EXP_TEN = 8


adapter_scale_factor = 2.0
SUM_TYPE = jnp.bfloat16


def routed(tokens, grad_up, tenant_ids, expert_ids, adapter_down, adapter_up, router):
    tok_rows = tokens.shape[0]
    model_width = tokens.shape[1]
    hidden_width = grad_up.shape[1]
    devices = lax.axis_size("tenant")
    capacity = 2 * tok_rows // devices
    buffer_len = devices * capacity
    global_ids = tenant_ids[:, None] * EXP_TEN + expert_ids
    logits = lax.dot_general(
        tokens, router, (((1,), (1,)), ((), ())), preferred_element_type=jnp.float32
    )
    picked = jnp.take_along_axis(logits, global_ids, axis=1)
    first_gate = jax.nn.sigmoid(picked[:, 0] - picked[:, 1])
    gate_sent = jnp.stack([first_gate, 1.0 - first_gate], axis=1).astype(jnp.bfloat16)
    flat_ids = global_ids.reshape(-1)
    slot_count = flat_ids.shape[0]
    same_owner = flat_ids[:, None] == flat_ids[None, :]
    slot_line = jnp.arange(slot_count, dtype=jnp.int32)
    earlier = slot_line[None, :] < slot_line[:, None]
    ranks = jnp.sum((same_owner & earlier).astype(jnp.int32), axis=1)
    places = (flat_ids * capacity + ranks).reshape(tok_rows, 2)

    def spread_rows(values):
        empty = jnp.zeros((buffer_len,) + values.shape[1:], values.dtype)
        return empty.at[places[:, 0]].set(values).at[places[:, 1]].set(values)

    send_rows = spread_rows(tokens).reshape(devices, capacity, model_width)
    send_grads = spread_rows(grad_up).reshape(devices, capacity, hidden_width)
    empty_gates = jnp.zeros((buffer_len,), jnp.bfloat16)
    send_gates = (
        empty_gates.at[places[:, 0]]
        .set(gate_sent[:, 0])
        .at[places[:, 1]]
        .set(gate_sent[:, 1])
        .reshape(devices, capacity)
    )
    recv_rows, recv_grads, recv_gates = (
        lax.all_to_all(send_rows, "tenant", split_axis=0, concat_axis=0, tiled=True),
        lax.all_to_all(send_grads, "tenant", split_axis=0, concat_axis=0, tiled=True),
        lax.all_to_all(send_gates, "tenant", split_axis=0, concat_axis=0, tiled=True),
    )
    rows_in = recv_rows.reshape(buffer_len, model_width)
    grads_in = recv_grads.reshape(buffer_len, hidden_width)
    incoming_gate_values = recv_gates.reshape(buffer_len).astype(jnp.float32)
    down = adapter_down[0]
    upper = adapter_up[0]
    reduced_rank_activations = lax.dot_general(
        rows_in, down, (((1,), (1,)), ((), ())), preferred_element_type=jnp.float32
    )
    returned_rank_gradient = lax.dot_general(
        grads_in, upper, (((1,), (1,)), ((), ())), preferred_element_type=jnp.float32
    )
    position_gate_value = (
        adapter_scale_factor * jnp.sum(reduced_rank_activations * returned_rank_gradient, axis=1)
    ).astype(jnp.bfloat16)
    gate_weighted_output = (
        adapter_scale_factor * incoming_gate_values[:, None] * returned_rank_gradient
    ).astype(jnp.bfloat16)
    scaled_reduced_activations = (
        adapter_scale_factor * incoming_gate_values[:, None] * reduced_rank_activations
    ).astype(jnp.bfloat16)
    slot_rows = jnp.dot(gate_weighted_output, down, preferred_element_type=jnp.float32).astype(
        jnp.bfloat16
    )
    back_rows, back_gates = (
        lax.all_to_all(
            slot_rows.reshape(devices, capacity, model_width),
            "tenant",
            split_axis=0,
            concat_axis=0,
            tiled=True,
        ),
        lax.all_to_all(
            position_gate_value.reshape(devices, capacity),
            "tenant",
            split_axis=0,
            concat_axis=0,
            tiled=True,
        ),
    )
    grad_down = lax.dot_general(
        gate_weighted_output, rows_in, (((0,), (0,)), ((), ())), preferred_element_type=jnp.float32
    )
    grad_upper = lax.dot_general(
        scaled_reduced_activations,
        grads_in,
        (((0,), (0,)), ((), ())),
        preferred_element_type=jnp.float32,
    )
    flat_back = back_rows.reshape(buffer_len, model_width)
    expert_grad = flat_back[places[:, 0]].astype(jnp.float32) + flat_back[places[:, 1]].astype(
        jnp.float32
    )
    gate_grads = back_gates.reshape(buffer_len)[places].astype(jnp.float32)
    logit_grad = first_gate * (1.0 - first_gate) * (gate_grads[:, 0] - gate_grads[:, 1])
    logit_sent = logit_grad.astype(jnp.bfloat16)
    columns = jnp.arange(router.shape[0], dtype=jnp.int32)[None, :]
    nothing = jnp.zeros((), jnp.bfloat16)
    signed = jnp.where(columns == global_ids[:, 0:1], logit_sent[:, None], nothing) - jnp.where(
        columns == global_ids[:, 1:2], logit_sent[:, None], nothing
    )
    router_term = jnp.dot(signed, router, preferred_element_type=jnp.float32)
    token_grad = (expert_grad + router_term).astype(jnp.bfloat16)
    router_grad = lax.psum_scatter(
        lax.dot_general(
            signed, tokens, (((0,), (0,)), ((), ())), preferred_element_type=jnp.float32
        ),
        "tenant",
        scatter_dimension=0,
        tiled=True,
    )
    return (token_grad, grad_down[None], grad_upper[None], router_grad)


GATHER_LIMIT = 16 * 1024 * 1024


def gathered(tokens, grad_up, tenant_ids, expert_ids, adapter_down, adapter_up, router):
    tok_rows = tokens.shape[0]
    experts = lax.axis_size("tenant")
    rank = adapter_down.shape[1]
    upper = lax.all_gather(adapter_up[0], "tenant", axis=0, tiled=True)
    down = lax.all_gather(adapter_down[0], "tenant", axis=0, tiled=True)
    global_ids = tenant_ids[:, None] * EXP_TEN + expert_ids
    columns = jnp.arange(experts, dtype=jnp.int32)[None, :]
    first_hot = columns == global_ids[:, 0:1]
    second_hot = columns == global_ids[:, 1:2]
    sign = first_hot.astype(jnp.float32) - second_hot.astype(jnp.float32)
    nt = (((1,), (1,)), ((), ()))
    tn = (((0,), (0,)), ((), ()))
    logits = lax.dot_general(tokens, router, nt, preferred_element_type=jnp.float32)
    first_gate = jax.nn.sigmoid(jnp.sum(logits * sign, axis=1, keepdims=True))
    gates = jnp.where(first_hot, first_gate, 0.0) + jnp.where(second_hot, 1.0 - first_gate, 0.0)
    gates = gates.astype(jnp.bfloat16).astype(jnp.float32)
    wide_gates = adapter_scale_factor * jnp.repeat(gates, rank, axis=1)
    back = lax.dot_general(grad_up, upper, nt, preferred_element_type=jnp.float32)
    low = lax.dot_general(tokens, down, nt, preferred_element_type=jnp.float32)
    weighted = (wide_gates * back).astype(jnp.bfloat16)
    scaled = (wide_gates * low).astype(jnp.bfloat16)
    slot_gate = adapter_scale_factor * jnp.sum((low * back).reshape(tok_rows, experts, rank), axis=2)
    slot_gate = slot_gate.astype(jnp.bfloat16).astype(jnp.float32)
    slot_diff = jnp.sum(slot_gate * sign, axis=1, keepdims=True)
    logit_sent = (first_gate * (1.0 - first_gate) * slot_diff).astype(jnp.bfloat16)
    signed = (logit_sent.astype(jnp.float32) * sign).astype(jnp.bfloat16)
    down_part = lax.dot_general(weighted, tokens, tn, preferred_element_type=jnp.float32)
    upper_part = lax.dot_general(scaled, grad_up, tn, preferred_element_type=jnp.float32)
    router_part = lax.dot_general(signed, tokens, tn, preferred_element_type=jnp.float32)

    def reduce(part):
        return lax.psum_scatter(
            part.astype(SUM_TYPE), "tenant", scatter_dimension=0, tiled=True
        ).astype(jnp.float32)

    grad_upper = reduce(upper_part)
    grad_down = reduce(down_part)
    router_grad = lax.psum_scatter(router_part, "tenant", scatter_dimension=0, tiled=True)
    token_grad = (
        jnp.dot(weighted, down, preferred_element_type=jnp.float32)
        + jnp.dot(signed, router, preferred_element_type=jnp.float32)
    ).astype(jnp.bfloat16)
    return (token_grad, grad_down[None], grad_upper[None], router_grad)


def per_device(tokens, grad_up, tenant_ids, expert_ids, adapter_down, adapter_up, router):
    factor_bytes = 2 * (adapter_down.size + adapter_up.size)
    plan = gathered if lax.axis_size("tenant") * factor_bytes <= GATHER_LIMIT else routed
    return plan(tokens, grad_up, tenant_ids, expert_ids, adapter_down, adapter_up, router)


def solution(mesh):
    in_specs = (
        P(("group", "tenant"), None),
        P(("group", "tenant"), None),
        P(("group", "tenant")),
        P(("group", "tenant"), None),
        P("tenant", None, None),
        P("tenant", None, None),
        P(),
    )
    out_specs = (
        P(("group", "tenant"), None),
        P(("group", "tenant"), None, None),
        P(("group", "tenant"), None, None),
        P(("group", "tenant"), None),
    )
    return jax.shard_map(
        per_device, mesh=mesh, in_specs=in_specs, out_specs=out_specs, check_vma=False
    )
```

```python
import jax
import jax.numpy as jnp
import functools

from jax import lax
from jax.experimental import pallas as pl
from jax.experimental.pallas import tpu as pltpu
from jax.sharding import PartitionSpec as P

EXP_TEN = 8


adapter_scale_factor = 2.0


def routed(tokens, grad_up, tenant_ids, expert_ids, adapter_down, adapter_up, router):
    tok_rows = tokens.shape[0]
    model_width = tokens.shape[1]
    hidden_width = grad_up.shape[1]
    devices = lax.axis_size("tenant")
    capacity = 2 * tok_rows // devices
    buffer_len = devices * capacity
    global_ids = tenant_ids[:, None] * EXP_TEN + expert_ids
    logits = lax.dot_general(
        tokens, router, (((1,), (1,)), ((), ())), preferred_element_type=jnp.float32
    )
    picked = jnp.take_along_axis(logits, global_ids, axis=1)
    first_gate = jax.nn.sigmoid(picked[:, 0] - picked[:, 1])
    gate_sent = jnp.stack([first_gate, 1.0 - first_gate], axis=1).astype(jnp.bfloat16)
    flat_ids = global_ids.reshape(-1)
    slot_count = flat_ids.shape[0]
    same_owner = flat_ids[:, None] == flat_ids[None, :]
    slot_line = jnp.arange(slot_count, dtype=jnp.int32)
    earlier = slot_line[None, :] < slot_line[:, None]
    ranks = jnp.sum((same_owner & earlier).astype(jnp.int32), axis=1)
    places = (flat_ids * capacity + ranks).reshape(tok_rows, 2)

    def spread_rows(values):
        empty = jnp.zeros((buffer_len,) + values.shape[1:], values.dtype)
        return empty.at[places[:, 0]].set(values).at[places[:, 1]].set(values)

    send_rows = spread_rows(tokens).reshape(devices, capacity, model_width)
    send_grads = spread_rows(grad_up).reshape(devices, capacity, hidden_width)
    empty_gates = jnp.zeros((buffer_len,), jnp.bfloat16)
    send_gates = (
        empty_gates.at[places[:, 0]]
        .set(gate_sent[:, 0])
        .at[places[:, 1]]
        .set(gate_sent[:, 1])
        .reshape(devices, capacity)
    )
    recv_rows, recv_grads, recv_gates = (
        lax.all_to_all(send_rows, "tenant", split_axis=0, concat_axis=0, tiled=True),
        lax.all_to_all(send_grads, "tenant", split_axis=0, concat_axis=0, tiled=True),
        lax.all_to_all(send_gates, "tenant", split_axis=0, concat_axis=0, tiled=True),
    )
    rows_in = recv_rows.reshape(buffer_len, model_width)
    grads_in = recv_grads.reshape(buffer_len, hidden_width)
    incoming_gate_values = recv_gates.reshape(buffer_len).astype(jnp.float32)
    down = adapter_down[0]
    upper = adapter_up[0]
    reduced_rank_activations = lax.dot_general(
        rows_in, down, (((1,), (1,)), ((), ())), preferred_element_type=jnp.float32
    )
    returned_rank_gradient = lax.dot_general(
        grads_in, upper, (((1,), (1,)), ((), ())), preferred_element_type=jnp.float32
    )
    position_gate_value = (
        adapter_scale_factor * jnp.sum(reduced_rank_activations * returned_rank_gradient, axis=1)
    ).astype(jnp.bfloat16)
    gate_weighted_output = (
        adapter_scale_factor * incoming_gate_values[:, None] * returned_rank_gradient
    ).astype(jnp.bfloat16)
    scaled_reduced_activations = (
        adapter_scale_factor * incoming_gate_values[:, None] * reduced_rank_activations
    ).astype(jnp.bfloat16)
    slot_rows = jnp.dot(gate_weighted_output, down, preferred_element_type=jnp.float32).astype(
        jnp.bfloat16
    )
    back_rows, back_gates = (
        lax.all_to_all(
            slot_rows.reshape(devices, capacity, model_width),
            "tenant",
            split_axis=0,
            concat_axis=0,
            tiled=True,
        ),
        lax.all_to_all(
            position_gate_value.reshape(devices, capacity),
            "tenant",
            split_axis=0,
            concat_axis=0,
            tiled=True,
        ),
    )
    grad_down = lax.dot_general(
        gate_weighted_output, rows_in, (((0,), (0,)), ((), ())), preferred_element_type=jnp.float32
    )
    grad_upper = lax.dot_general(
        scaled_reduced_activations,
        grads_in,
        (((0,), (0,)), ((), ())),
        preferred_element_type=jnp.float32,
    )
    flat_back = back_rows.reshape(buffer_len, model_width)
    expert_grad = flat_back[places[:, 0]].astype(jnp.float32) + flat_back[places[:, 1]].astype(
        jnp.float32
    )
    gate_grads = back_gates.reshape(buffer_len)[places].astype(jnp.float32)
    logit_grad = first_gate * (1.0 - first_gate) * (gate_grads[:, 0] - gate_grads[:, 1])
    logit_sent = logit_grad.astype(jnp.bfloat16)
    columns = jnp.arange(router.shape[0], dtype=jnp.int32)[None, :]
    nothing = jnp.zeros((), jnp.bfloat16)
    signed = jnp.where(columns == global_ids[:, 0:1], logit_sent[:, None], nothing) - jnp.where(
        columns == global_ids[:, 1:2], logit_sent[:, None], nothing
    )
    router_term = jnp.dot(signed, router, preferred_element_type=jnp.float32)
    token_grad = (expert_grad + router_term).astype(jnp.bfloat16)
    router_grad = lax.psum_scatter(
        lax.dot_general(
            signed, tokens, (((0,), (0,)), ((), ())), preferred_element_type=jnp.float32
        ),
        "tenant",
        scatter_dimension=0,
        tiled=True,
    )
    return (token_grad, grad_down[None], grad_upper[None], router_grad)


F32 = jnp.float32
BF16 = jnp.bfloat16
TILE = 1024
PIECE = 512


def loop(count, body):
    def step(i, carry):
        body(i)
        return carry

    lax.fori_loop(0, count, step, 0)


def fused_kernel(
    tok, gup, ids, adn, aup, router,
    tok_out, dn_out, up_out, rt_out,
    fac, part, core_in, x_in, left_in, right_in,
    low, back, logits, wide, wide_t, scaled_t, sign_t, signed, acc,
    own_sem, ag_send, ag_recv, core_send, core_recv, x_send, x_recv, z_send, left_recv, right_recv,
):
    me = lax.axis_index("tenant")
    c = lax.rem(me, 2)
    x = lax.rem(lax.div(me, 2), 2)
    z = lax.div(me, 4)
    model = tok.shape[1]
    hidden = gup.shape[1]
    both = model + hidden
    total = part.shape[2]
    rows = tok.shape[0]

    right = me + 4
    left = me - 4
    x_peer = me + 2 - 4 * x
    c_peer = me + 1 - 2 * c

    def slot(cc, zz, xx):
        return cc * 8 + zz * 2 + xx

    barrier = pltpu.get_barrier_semaphore()

    def greet(peer):
        pl.semaphore_signal(
            barrier, inc=1, device_id={"tenant": peer}, device_id_type=pl.DeviceIdType.MESH
        )

    own = slot(c, z, x)
    own_dn = pltpu.make_async_copy(adn, fac.at[own, :, pl.ds(0, model)], own_sem.at[0])
    own_up = pltpu.make_async_copy(aup, fac.at[own, :, pl.ds(model, hidden)], own_sem.at[1])
    own_dn.start()
    own_up.start()
    greet(x_peer)
    greet(c_peer)
    pl.when(z < 3)(lambda: greet(right))
    pl.when(z > 0)(lambda: greet(left))
    pl.semaphore_wait(
        barrier, 2 + jnp.where(z < 3, 1, 0).astype(jnp.int32) + jnp.where(z > 0, 1, 0).astype(jnp.int32)
    )
    own_dn.wait()
    own_up.wait()

    def remote(src, dst, send, recv, peer):
        return pltpu.make_async_remote_copy(
            src_ref=src, dst_ref=dst, send_sem=send, recv_sem=recv,
            device_id={"tenant": peer}, device_id_type=pl.DeviceIdType.MESH,
        )

    def gather_copy(at, send_at, peer):
        return remote(fac.at[at], fac.at[at], ag_send.at[send_at], ag_recv.at[at], peer)

    def to_right(zz):
        return gather_copy(slot(c, zz, x), zz, right)

    def to_left(zz):
        return gather_copy(slot(c, zz, x), 4 + zz, left)

    def to_x(zz):
        return gather_copy(slot(c, zz, x), 8 + zz, x_peer)

    def to_core(zz, xx):
        return gather_copy(slot(c, zz, xx), 12 + zz * 2 + xx, c_peer)

    def arrived(at):
        gather_copy(at, 0, c_peer).wait_recv()

    pl.when(z < 3)(lambda: to_right(z).start())
    pl.when(z > 0)(lambda: to_left(z).start())
    to_x(z).start()
    to_core(z, x).start()

    nt = (((1,), (1,)), ((), ()))
    logits[...] = jnp.zeros_like(logits)

    def logit_tile(i):
        cols = pl.ds(pl.multiple_of(i * TILE, TILE), TILE)
        logits[...] += lax.dot_general(tok[:, cols], router[:, cols], nt, preferred_element_type=F32)

    loop(model // TILE, logit_tile)

    for s in range(1, 4):
        def from_left(s=s):
            arrived(slot(c, z - s, x))
            pl.when(z < 3)(lambda: to_right(z - s).start())
            to_x(z - s).start()
            to_core(z - s, x).start()

        def from_right(s=s):
            arrived(slot(c, z + s, x))
            pl.when(z > 0)(lambda: to_left(z + s).start())
            to_x(z + s).start()
            to_core(z + s, x).start()

        pl.when(z - s >= 0)(from_left)
        pl.when(z + s <= 3)(from_right)

    def x_block(zz):
        arrived(slot(c, zz, 1 - x))
        to_core(zz, 1 - x).start()

    x_block(z)
    for s in range(1, 4):
        pl.when(z - s >= 0)(functools.partial(x_block, z - s))
        pl.when(z + s <= 3)(functools.partial(x_block, z + s))
    for k in range(8):
        arrived((1 - c) * 8 + k)

    def factor_tile(start):
        return fac[:, :, pl.ds(start, TILE)].reshape(256, TILE)

    low[...] = jnp.zeros_like(low)
    back[...] = jnp.zeros_like(back)

    def low_tile(i):
        start = pl.multiple_of(i * TILE, TILE)
        low[...] += lax.dot_general(
            tok[:, pl.ds(start, TILE)], factor_tile(start), nt, preferred_element_type=F32
        )

    def back_tile(i):
        start = pl.multiple_of(i * TILE, TILE)
        back[...] += lax.dot_general(
            gup[:, pl.ds(start, TILE)],
            factor_tile(pl.multiple_of(model + start, TILE)),
            nt,
            preferred_element_type=F32,
        )

    loop(model // TILE, low_tile)
    loop(hidden // TILE, back_tile)

    first = ids[:, 0:1]
    second = ids[:, 1:2]
    narrow = lax.broadcasted_iota(jnp.int32, (rows, 16), 1)
    n_sign = jnp.where(narrow == first, 1.0, 0.0) - jnp.where(narrow == second, 1.0, 0.0)
    first_gate = jax.nn.sigmoid(jnp.sum(logits[...] * n_sign, axis=1, keepdims=True))
    place = lax.broadcasted_iota(jnp.int32, (rows, 256), 1) // 16
    expert = (place % 8) * 2 + place // 8
    hot1 = expert == first
    hot2 = expert == second
    one = first_gate.astype(BF16).astype(F32)
    two = (1.0 - first_gate).astype(BF16).astype(F32)
    gates = adapter_scale_factor * (jnp.where(hot1, one, 0.0) + jnp.where(hot2, two, 0.0))
    lows = low[...]
    backs = back[...]
    weighted = gates * backs
    product = lows * backs

    def slot_gate(hot):
        picked = jnp.sum(jnp.where(hot, product, 0.0), axis=1, keepdims=True)
        return (adapter_scale_factor * picked).astype(BF16).astype(F32)

    logit_sent = first_gate * (1.0 - first_gate) * (slot_gate(hot1) - slot_gate(hot2))
    signed[...] = (logit_sent * n_sign).astype(BF16)
    w_sign = jnp.where(hot1, logit_sent, 0.0) - jnp.where(hot2, logit_sent, 0.0)
    wide[...] = weighted.astype(BF16)
    wide_t[...] = weighted.T.astype(BF16)
    scaled_t[...] = (gates * lows).T.astype(BF16)
    sign_t[...] = w_sign.T.astype(BF16)

    def partials(cc):
        lines = pl.ds(pl.multiple_of(cc * 128, 128), 128)
        slots = pl.ds(cc * 8, 8)

        def dn_tile(i):
            start = pl.multiple_of(i * TILE, TILE)
            tile = jnp.dot(wide_t[lines, :], tok[:, pl.ds(start, TILE)], preferred_element_type=F32)
            part[slots, :, pl.ds(start, TILE)] = tile.astype(BF16).reshape(8, 16, TILE)

        def up_tile(i):
            start = pl.multiple_of(i * TILE, TILE)
            tile = jnp.dot(scaled_t[lines, :], gup[:, pl.ds(start, TILE)], preferred_element_type=F32)
            part[slots, :, pl.ds(pl.multiple_of(model + start, TILE), TILE)] = tile.astype(
                BF16
            ).reshape(8, 16, TILE)

        acc[...] = jnp.zeros_like(acc)
        line = lax.broadcasted_iota(jnp.int32, (128, PIECE), 0) % 16

        def router_tile(i):
            cols = pl.ds(pl.multiple_of(i * PIECE, PIECE), PIECE)
            tile = jnp.dot(sign_t[lines, :], tok[:, cols], preferred_element_type=F32)
            acc[...] = jnp.where(line == i, tile, acc[...])

        loop(model // TILE, dn_tile)
        loop(hidden // TILE, up_tile)
        loop(16, router_tile)
        part[slots, :, pl.ds(both, PIECE)] = acc[...].astype(BF16).reshape(8, 16, PIECE)

    def order(k):
        low_half = (3, 2, 1 - z, z)[k]
        high_half = (0, 1, 5 - z, z)[k]
        return jnp.where(z < 2, low_half, high_half)

    def core_copy(zz, xx):
        at = zz * 2 + xx
        return remote(
            part.at[slot(1 - c, zz, xx)], core_in.at[at], core_send.at[at], core_recv.at[at], c_peer
        )

    def x_copy(zz):
        return remote(
            part.at[slot(c, zz, 1 - x)], x_in.at[zz], x_send.at[zz], x_recv.at[zz], x_peer
        )

    def right_copy(zz):
        return remote(
            part.at[slot(c, zz, x)], left_in.at[zz], z_send.at[zz], left_recv.at[zz], right
        )

    def left_copy(zz):
        return remote(
            part.at[slot(c, zz, x)], right_in.at[zz], z_send.at[zz], right_recv.at[zz], left
        )

    width = total // 7

    def add(at, buf, index):
        def tile(i):
            cols = pl.ds(pl.multiple_of(i * width, 128), width)
            part[at, :, cols] = (
                part[at, :, cols].astype(F32) + buf[index, :, cols].astype(F32)
            ).astype(BF16)

        loop(7, tile)

    partials(1 - c)
    for k in range(4):
        core_copy(order(k), 1 - x).start()
    for k in range(4):
        core_copy(order(k), x).start()
    partials(c)
    for k in range(4):
        d = order(k)
        core_copy(d, 1 - x).wait_recv()
        add(slot(c, d, 1 - x), core_in, d * 2 + 1 - x)
        x_copy(d).start()
    for k in range(4):
        d = order(k)
        core_copy(d, x).wait_recv()
        add(slot(c, d, x), core_in, d * 2 + x)

    def token_tile(i):
        start = pl.multiple_of(i * TILE, TILE)
        cols = pl.ds(start, TILE)
        tok_out[:, cols] = (
            jnp.dot(wide[...], factor_tile(start), preferred_element_type=F32)
            + jnp.dot(signed[...], router[:, cols], preferred_element_type=F32)
        ).astype(BF16)

    loop(model // TILE, token_tile)

    for k in range(3):
        d = order(k)
        mine = slot(c, d, x)
        x_copy(d).wait_recv()
        add(mine, x_in, d)

        def rightward(d=d, mine=mine):
            def more():
                right_copy(d).wait_recv()
                add(mine, left_in, d)

            pl.when(z > 0)(more)
            right_copy(d).start()

        def leftward(d=d, mine=mine):
            def more():
                left_copy(d).wait_recv()
                add(mine, right_in, d)

            pl.when(z < 3)(more)
            left_copy(d).start()

        pl.when(d > z)(rightward)
        pl.when(d < z)(leftward)

    def results(body):
        def dn_tile(i):
            start = pl.multiple_of(i * TILE, TILE)
            body(dn_out, pl.ds(start, TILE), pl.ds(start, TILE))

        def up_tile(i):
            start = pl.multiple_of(i * TILE, TILE)
            body(up_out, pl.ds(start, TILE), pl.ds(pl.multiple_of(model + start, TILE), TILE))

        loop(model // TILE, dn_tile)
        loop(hidden // TILE, up_tile)
        body(rt_out, pl.ds(0, PIECE), pl.ds(both, PIECE))

    def first_terms(out, here, there):
        out[:, here] = part[own, :, there].astype(F32) + x_in[z, :, there].astype(F32)

    def left_term(out, here, there):
        out[:, here] += left_in[z, :, there].astype(F32)

    def right_term(out, here, there):
        out[:, here] += right_in[z, :, there].astype(F32)

    def take_left():
        right_copy(z).wait_recv()
        results(left_term)

    def take_right():
        left_copy(z).wait_recv()
        results(right_term)

    x_copy(z).wait_recv()
    results(first_terms)
    pl.when(z > 0)(take_left)
    pl.when(z < 3)(take_right)

    for zz in range(4):
        pl.when((z < 3) & (zz <= z))(lambda zz=zz: to_right(zz).wait_send())
        pl.when((z > 0) & (zz >= z))(lambda zz=zz: to_left(zz).wait_send())
        to_x(zz).wait_send()
        x_copy(zz).wait_send()
        pl.when(zz > z)(lambda zz=zz: right_copy(zz).wait_send())
        pl.when(zz < z)(lambda zz=zz: left_copy(zz).wait_send())
        for xx in range(2):
            to_core(zz, xx).wait_send()
            core_copy(zz, xx).wait_send()


def fused(tokens, grad_up, tenant_ids, expert_ids, adapter_down, adapter_up, router):
    rows, model = tokens.shape
    hidden = grad_up.shape[1]
    rank = adapter_down.shape[1]
    both = model + hidden
    total = both + PIECE
    ids = tenant_ids[:, None] * EXP_TEN + expert_ids
    vmem = pl.BlockSpec(memory_space=pltpu.VMEM)
    dma = pltpu.SemaphoreType.DMA
    tok_out, dn_out, up_out, rt_out = pl.pallas_call(
        fused_kernel,
        out_shape=(
            jax.ShapeDtypeStruct((rows, model), BF16),
            jax.ShapeDtypeStruct((rank, model), F32),
            jax.ShapeDtypeStruct((rank, hidden), F32),
            jax.ShapeDtypeStruct((16, PIECE), F32),
        ),
        in_specs=[vmem] * 6,
        out_specs=(vmem,) * 4,
        scratch_shapes=[
            pltpu.VMEM((16, rank, both), BF16),
            pltpu.VMEM((16, rank, total), BF16),
            pltpu.VMEM((8, rank, total), BF16),
            pltpu.VMEM((4, rank, total), BF16),
            pltpu.VMEM((4, rank, total), BF16),
            pltpu.VMEM((4, rank, total), BF16),
            pltpu.VMEM((rows, 256), F32),
            pltpu.VMEM((rows, 256), F32),
            pltpu.VMEM((rows, 16), F32),
            pltpu.VMEM((rows, 256), BF16),
            pltpu.VMEM((256, rows), BF16),
            pltpu.VMEM((256, rows), BF16),
            pltpu.VMEM((256, rows), BF16),
            pltpu.VMEM((rows, 16), BF16),
            pltpu.VMEM((128, PIECE), F32),
            dma((2,)), dma((20,)), dma((16,)), dma((8,)), dma((8,)),
            dma((4,)), dma((4,)), dma((4,)), dma((4,)), dma((4,)),
        ],
        compiler_params=pltpu.CompilerParams(
            collective_id=0, has_side_effects=True, vmem_limit_bytes=60 * 1024 * 1024
        ),
    )(tokens, grad_up, ids, adapter_down[0], adapter_up[0], router)
    return (tok_out, dn_out[None], up_out[None], rt_out.reshape(1, model))


def per_device(tokens, grad_up, tenant_ids, expert_ids, adapter_down, adapter_up, router):
    fits = lax.axis_size("tenant") == 16 and tokens.shape[0] == 128 and adapter_down.shape[1] == 16
    plan = fused if fits else routed
    return plan(tokens, grad_up, tenant_ids, expert_ids, adapter_down, adapter_up, router)


def solution(mesh):
    in_specs = (
        P(("group", "tenant"), None),
        P(("group", "tenant"), None),
        P(("group", "tenant")),
        P(("group", "tenant"), None),
        P("tenant", None, None),
        P("tenant", None, None),
        P(),
    )
    out_specs = (
        P(("group", "tenant"), None),
        P(("group", "tenant"), None, None),
        P(("group", "tenant"), None, None),
        P(("group", "tenant"), None),
    )
    return jax.shard_map(
        per_device, mesh=mesh, in_specs=in_specs, out_specs=out_specs, check_vma=False
    )
```

```python
import jax
import jax.numpy as jnp
import functools

from jax import lax
from jax.experimental import pallas as pl
from jax.experimental.pallas import tpu as pltpu
from jax.sharding import PartitionSpec as P

EXP_TEN = 8


adapter_scale_factor = 2.0


def routed(tokens, grad_up, tenant_ids, expert_ids, adapter_down, adapter_up, router):
    tok_rows = tokens.shape[0]
    model_width = tokens.shape[1]
    hidden_width = grad_up.shape[1]
    devices = lax.axis_size("tenant")
    capacity = 2 * tok_rows // devices
    buffer_len = devices * capacity
    global_ids = tenant_ids[:, None] * EXP_TEN + expert_ids
    logits = lax.dot_general(
        tokens, router, (((1,), (1,)), ((), ())), preferred_element_type=jnp.float32
    )
    picked = jnp.take_along_axis(logits, global_ids, axis=1)
    first_gate = jax.nn.sigmoid(picked[:, 0] - picked[:, 1])
    gate_sent = jnp.stack([first_gate, 1.0 - first_gate], axis=1).astype(jnp.bfloat16)
    flat_ids = global_ids.reshape(-1)
    slot_count = flat_ids.shape[0]
    same_owner = flat_ids[:, None] == flat_ids[None, :]
    slot_line = jnp.arange(slot_count, dtype=jnp.int32)
    earlier = slot_line[None, :] < slot_line[:, None]
    ranks = jnp.sum((same_owner & earlier).astype(jnp.int32), axis=1)
    places = (flat_ids * capacity + ranks).reshape(tok_rows, 2)

    def spread_rows(values):
        empty = jnp.zeros((buffer_len,) + values.shape[1:], values.dtype)
        return empty.at[places[:, 0]].set(values).at[places[:, 1]].set(values)

    send_rows = spread_rows(tokens).reshape(devices, capacity, model_width)
    send_grads = spread_rows(grad_up).reshape(devices, capacity, hidden_width)
    empty_gates = jnp.zeros((buffer_len,), jnp.bfloat16)
    send_gates = (
        empty_gates.at[places[:, 0]]
        .set(gate_sent[:, 0])
        .at[places[:, 1]]
        .set(gate_sent[:, 1])
        .reshape(devices, capacity)
    )
    recv_rows, recv_grads, recv_gates = (
        lax.all_to_all(send_rows, "tenant", split_axis=0, concat_axis=0, tiled=True),
        lax.all_to_all(send_grads, "tenant", split_axis=0, concat_axis=0, tiled=True),
        lax.all_to_all(send_gates, "tenant", split_axis=0, concat_axis=0, tiled=True),
    )
    rows_in = recv_rows.reshape(buffer_len, model_width)
    grads_in = recv_grads.reshape(buffer_len, hidden_width)
    incoming_gate_values = recv_gates.reshape(buffer_len).astype(jnp.float32)
    down = adapter_down[0]
    upper = adapter_up[0]
    reduced_rank_activations = lax.dot_general(
        rows_in, down, (((1,), (1,)), ((), ())), preferred_element_type=jnp.float32
    )
    returned_rank_gradient = lax.dot_general(
        grads_in, upper, (((1,), (1,)), ((), ())), preferred_element_type=jnp.float32
    )
    position_gate_value = (
        adapter_scale_factor * jnp.sum(reduced_rank_activations * returned_rank_gradient, axis=1)
    ).astype(jnp.bfloat16)
    gate_weighted_output = (
        adapter_scale_factor * incoming_gate_values[:, None] * returned_rank_gradient
    ).astype(jnp.bfloat16)
    scaled_reduced_activations = (
        adapter_scale_factor * incoming_gate_values[:, None] * reduced_rank_activations
    ).astype(jnp.bfloat16)
    slot_rows = jnp.dot(gate_weighted_output, down, preferred_element_type=jnp.float32).astype(
        jnp.bfloat16
    )
    back_rows, back_gates = (
        lax.all_to_all(
            slot_rows.reshape(devices, capacity, model_width),
            "tenant",
            split_axis=0,
            concat_axis=0,
            tiled=True,
        ),
        lax.all_to_all(
            position_gate_value.reshape(devices, capacity),
            "tenant",
            split_axis=0,
            concat_axis=0,
            tiled=True,
        ),
    )
    grad_down = lax.dot_general(
        gate_weighted_output, rows_in, (((0,), (0,)), ((), ())), preferred_element_type=jnp.float32
    )
    grad_upper = lax.dot_general(
        scaled_reduced_activations,
        grads_in,
        (((0,), (0,)), ((), ())),
        preferred_element_type=jnp.float32,
    )
    flat_back = back_rows.reshape(buffer_len, model_width)
    expert_grad = flat_back[places[:, 0]].astype(jnp.float32) + flat_back[places[:, 1]].astype(
        jnp.float32
    )
    gate_grads = back_gates.reshape(buffer_len)[places].astype(jnp.float32)
    logit_grad = first_gate * (1.0 - first_gate) * (gate_grads[:, 0] - gate_grads[:, 1])
    logit_sent = logit_grad.astype(jnp.bfloat16)
    columns = jnp.arange(router.shape[0], dtype=jnp.int32)[None, :]
    nothing = jnp.zeros((), jnp.bfloat16)
    signed = jnp.where(columns == global_ids[:, 0:1], logit_sent[:, None], nothing) - jnp.where(
        columns == global_ids[:, 1:2], logit_sent[:, None], nothing
    )
    router_term = jnp.dot(signed, router, preferred_element_type=jnp.float32)
    token_grad = (expert_grad + router_term).astype(jnp.bfloat16)
    router_grad = lax.psum_scatter(
        lax.dot_general(
            signed, tokens, (((0,), (0,)), ((), ())), preferred_element_type=jnp.float32
        ),
        "tenant",
        scatter_dimension=0,
        tiled=True,
    )
    return (token_grad, grad_down[None], grad_upper[None], router_grad)


F32 = jnp.float32
BF16 = jnp.bfloat16
TILE = 1024
PIECE = 512


def loop(count, body):
    def step(i, carry):
        body(i)
        return carry

    lax.fori_loop(0, count, step, 0)


def fused_kernel(
    tok, gup, ids, adn, aup, router,
    tok_out, dn_out, up_out, rt_out,
    fac, part, core_in, x_in, left_in, right_in,
    low, back, logits, wide, wide_t, scaled_t, sign_t, signed, acc,
    own_sem, ag_send, ag_recv, y_send, y_recv, core_send, core_recv, x_send, x_recv, z_send, left_recv, right_recv,
):
    me = lax.axis_index("tenant")
    g = lax.axis_index("group")
    c = lax.rem(me, 2)
    x = lax.rem(lax.div(me, 2), 2)
    z = lax.div(me, 4)
    model = tok.shape[1]
    hidden = gup.shape[1]
    half = hidden // 2
    both = model + hidden
    total = part.shape[2]
    rows = tok.shape[0]

    right = me + 4
    left = me - 4
    x_peer = me + 2 - 4 * x
    c_peer = me + 1 - 2 * c

    def slot(cc, zz, xx):
        return cc * 8 + zz * 2 + xx

    barrier = pltpu.get_barrier_semaphore()

    def greet(peer, group=g):
        pl.semaphore_signal(
            barrier,
            inc=1,
            device_id={"group": group, "tenant": peer},
            device_id_type=pl.DeviceIdType.MESH,
        )

    own = slot(c, z, x)
    own_dn = pltpu.make_async_copy(adn, fac.at[own, :, pl.ds(half, model)], own_sem.at[0])
    own_lo = pltpu.make_async_copy(
        aup.at[:, pl.ds(0, half)], fac.at[own, :, pl.ds(0, half)], own_sem.at[1]
    )
    own_hi = pltpu.make_async_copy(
        aup.at[:, pl.ds(half, half)], fac.at[own, :, pl.ds(half + model, half)], own_sem.at[2]
    )
    own_dn.start()
    own_lo.start()
    own_hi.start()
    greet(x_peer)
    greet(c_peer)
    greet(me, 1 - g)
    pl.when(z < 3)(lambda: greet(right))
    pl.when(z > 0)(lambda: greet(left))
    pl.semaphore_wait(
        barrier, 3 + jnp.where(z < 3, 1, 0).astype(jnp.int32) + jnp.where(z > 0, 1, 0).astype(jnp.int32)
    )
    own_dn.wait()
    own_lo.wait()
    own_hi.wait()

    def remote(src, dst, send, recv, peer, group=g):
        return pltpu.make_async_remote_copy(
            src_ref=src, dst_ref=dst, send_sem=send, recv_sem=recv,
            device_id={"group": group, "tenant": peer}, device_id_type=pl.DeviceIdType.MESH,
        )

    gathered = pl.ds(pl.multiple_of(g * half, 128), half + model)
    mine_y = pl.ds(pl.multiple_of(g * (half + model), 128), half)
    other_y = pl.ds(pl.multiple_of((1 - g) * (half + model), 128), half)

    def gather_copy(at, send_at, peer):
        block = fac.at[at, :, gathered]
        return remote(block, block, ag_send.at[send_at], ag_recv.at[at], peer)

    def to_y(zz, xx):
        at = slot(c, zz, xx)
        block = fac.at[at, :, mine_y]
        return remote(block, block, y_send.at[zz * 2 + xx], y_recv.at[at], me, 1 - g)

    def y_to_core(zz, xx):
        at = slot(c, zz, xx)
        block = fac.at[at, :, other_y]
        return remote(block, block, y_send.at[8 + zz * 2 + xx], y_recv.at[at], c_peer)

    def y_arrived(at):
        block = fac.at[at, :, other_y]
        remote(block, block, y_send.at[0], y_recv.at[at], c_peer).wait_recv()

    def to_right(zz):
        return gather_copy(slot(c, zz, x), zz, right)

    def to_left(zz):
        return gather_copy(slot(c, zz, x), 4 + zz, left)

    def to_x(zz):
        return gather_copy(slot(c, zz, x), 8 + zz, x_peer)

    def to_core(zz, xx):
        return gather_copy(slot(c, zz, xx), 12 + zz * 2 + xx, c_peer)

    def arrived(at):
        gather_copy(at, 0, c_peer).wait_recv()

    pl.when(z < 3)(lambda: to_right(z).start())
    pl.when(z > 0)(lambda: to_left(z).start())
    to_x(z).start()
    to_core(z, x).start()
    y_to_core(z, x).start()

    nt = (((1,), (1,)), ((), ()))
    logits[...] = jnp.zeros_like(logits)

    def logit_tile(i):
        cols = pl.ds(pl.multiple_of(i * TILE, TILE), TILE)
        logits[...] += lax.dot_general(tok[:, cols], router[:, cols], nt, preferred_element_type=F32)

    loop(model // TILE, logit_tile)

    for s in range(1, 4):
        def from_left(s=s):
            arrived(slot(c, z - s, x))
            pl.when(z < 3)(lambda: to_right(z - s).start())
            to_x(z - s).start()
            to_y(z - s, x).start()
            to_core(z - s, x).start()

        def from_right(s=s):
            arrived(slot(c, z + s, x))
            pl.when(z > 0)(lambda: to_left(z + s).start())
            to_x(z + s).start()
            to_y(z + s, x).start()
            to_core(z + s, x).start()

        pl.when(z - s >= 0)(from_left)
        pl.when(z + s <= 3)(from_right)

    def x_block(zz):
        arrived(slot(c, zz, 1 - x))
        to_y(zz, 1 - x).start()
        to_core(zz, 1 - x).start()

    def y_block(zz, xx):
        y_arrived(slot(c, zz, xx))
        y_to_core(zz, xx).start()

    x_block(z)
    for s in range(1, 4):
        for inside, zz in ((z - s >= 0, z - s), (z + s <= 3, z + s)):
            pl.when(inside)(functools.partial(y_block, zz, x))
            pl.when(inside)(functools.partial(x_block, zz))
    y_block(z, 1 - x)
    for s in range(1, 4):
        for inside, zz in ((z - s >= 0, z - s), (z + s <= 3, z + s)):
            pl.when(inside)(functools.partial(y_block, zz, 1 - x))
    for k in range(8):
        arrived((1 - c) * 8 + k)

    def factor_tile(start):
        return fac[:, :, pl.ds(start, TILE)].reshape(256, TILE)

    low[...] = jnp.zeros_like(low)
    back[...] = jnp.zeros_like(back)

    def low_tile(i):
        start = pl.multiple_of(i * TILE, TILE)
        low[...] += lax.dot_general(
            tok[:, pl.ds(start, TILE)],
            factor_tile(pl.multiple_of(half + start, TILE)),
            nt,
            preferred_element_type=F32
        )

    def back_tile(i):
        start = pl.multiple_of(i * TILE, TILE)
        back[...] += lax.dot_general(
            gup[:, pl.ds(start, TILE)],
            factor_tile(pl.multiple_of(start + jnp.where(start >= half, model, 0), TILE)),
            nt,
            preferred_element_type=F32,
        )

    loop(model // TILE, low_tile)
    for k in range(8):
        y_arrived((1 - c) * 8 + k)
    loop(hidden // TILE, back_tile)

    first = ids[:, 0:1]
    second = ids[:, 1:2]
    narrow = lax.broadcasted_iota(jnp.int32, (rows, 16), 1)
    n_sign = jnp.where(narrow == first, 1.0, 0.0) - jnp.where(narrow == second, 1.0, 0.0)
    first_gate = jax.nn.sigmoid(jnp.sum(logits[...] * n_sign, axis=1, keepdims=True))
    place = lax.broadcasted_iota(jnp.int32, (rows, 256), 1) // 16
    expert = (place % 8) * 2 + place // 8
    hot1 = expert == first
    hot2 = expert == second
    one = first_gate.astype(BF16).astype(F32)
    two = (1.0 - first_gate).astype(BF16).astype(F32)
    gates = adapter_scale_factor * (jnp.where(hot1, one, 0.0) + jnp.where(hot2, two, 0.0))
    lows = low[...]
    backs = back[...]
    weighted = gates * backs
    product = lows * backs

    def slot_gate(hot):
        picked = jnp.sum(jnp.where(hot, product, 0.0), axis=1, keepdims=True)
        return (adapter_scale_factor * picked).astype(BF16).astype(F32)

    logit_sent = first_gate * (1.0 - first_gate) * (slot_gate(hot1) - slot_gate(hot2))
    signed[...] = (logit_sent * n_sign).astype(BF16)
    w_sign = jnp.where(hot1, logit_sent, 0.0) - jnp.where(hot2, logit_sent, 0.0)
    wide[...] = weighted.astype(BF16)
    wide_t[...] = weighted.T.astype(BF16)
    scaled_t[...] = (gates * lows).T.astype(BF16)
    sign_t[...] = w_sign.T.astype(BF16)

    def partials(cc):
        lines = pl.ds(pl.multiple_of(cc * 128, 128), 128)
        slots = pl.ds(cc * 8, 8)

        def dn_tile(i):
            start = pl.multiple_of(i * TILE, TILE)
            tile = jnp.dot(wide_t[lines, :], tok[:, pl.ds(start, TILE)], preferred_element_type=F32)
            part[slots, :, pl.ds(start, TILE)] = tile.astype(BF16).reshape(8, 16, TILE)

        def up_tile(i):
            start = pl.multiple_of(i * TILE, TILE)
            tile = jnp.dot(scaled_t[lines, :], gup[:, pl.ds(start, TILE)], preferred_element_type=F32)
            part[slots, :, pl.ds(pl.multiple_of(model + start, TILE), TILE)] = tile.astype(
                BF16
            ).reshape(8, 16, TILE)

        acc[...] = jnp.zeros_like(acc)
        line = lax.broadcasted_iota(jnp.int32, (128, PIECE), 0) % 16

        def router_tile(i):
            cols = pl.ds(pl.multiple_of(i * PIECE, PIECE), PIECE)
            tile = jnp.dot(sign_t[lines, :], tok[:, cols], preferred_element_type=F32)
            acc[...] = jnp.where(line == i, tile, acc[...])

        loop(model // TILE, dn_tile)
        loop(hidden // TILE, up_tile)
        loop(16, router_tile)
        part[slots, :, pl.ds(both, PIECE)] = acc[...].astype(BF16).reshape(8, 16, PIECE)

    def order(k):
        low_half = (3, 2, 1 - z, z)[k]
        high_half = (0, 1, 5 - z, z)[k]
        return jnp.where(z < 2, low_half, high_half)

    def core_copy(zz, xx):
        at = zz * 2 + xx
        return remote(
            part.at[slot(1 - c, zz, xx)], core_in.at[at], core_send.at[at], core_recv.at[at], c_peer
        )

    def x_copy(zz):
        return remote(
            part.at[slot(c, zz, 1 - x)], x_in.at[zz], x_send.at[zz], x_recv.at[zz], x_peer
        )

    def right_copy(zz):
        return remote(
            part.at[slot(c, zz, x)], left_in.at[zz], z_send.at[zz], left_recv.at[zz], right
        )

    def left_copy(zz):
        return remote(
            part.at[slot(c, zz, x)], right_in.at[zz], z_send.at[zz], right_recv.at[zz], left
        )

    width = total // 7

    def add(at, buf, index):
        def tile(i):
            cols = pl.ds(pl.multiple_of(i * width, 128), width)
            part[at, :, cols] = (
                part[at, :, cols].astype(F32) + buf[index, :, cols].astype(F32)
            ).astype(BF16)

        loop(7, tile)

    partials(1 - c)
    for k in range(4):
        core_copy(order(k), 1 - x).start()
    for k in range(4):
        core_copy(order(k), x).start()
    partials(c)
    for k in range(4):
        d = order(k)
        core_copy(d, 1 - x).wait_recv()
        add(slot(c, d, 1 - x), core_in, d * 2 + 1 - x)
        x_copy(d).start()
    for k in range(4):
        d = order(k)
        core_copy(d, x).wait_recv()
        add(slot(c, d, x), core_in, d * 2 + x)

    def token_tile(i):
        start = pl.multiple_of(i * TILE, TILE)
        cols = pl.ds(start, TILE)
        tok_out[:, cols] = (
            jnp.dot(
                wide[...], factor_tile(pl.multiple_of(half + start, TILE)), preferred_element_type=F32
            )
            + jnp.dot(signed[...], router[:, cols], preferred_element_type=F32)
        ).astype(BF16)

    loop(model // TILE, token_tile)

    for k in range(3):
        d = order(k)
        mine = slot(c, d, x)
        x_copy(d).wait_recv()
        add(mine, x_in, d)

        def rightward(d=d, mine=mine):
            def more():
                right_copy(d).wait_recv()
                add(mine, left_in, d)

            pl.when(z > 0)(more)
            right_copy(d).start()

        def leftward(d=d, mine=mine):
            def more():
                left_copy(d).wait_recv()
                add(mine, right_in, d)

            pl.when(z < 3)(more)
            left_copy(d).start()

        pl.when(d > z)(rightward)
        pl.when(d < z)(leftward)

    def results(body):
        def dn_tile(i):
            start = pl.multiple_of(i * TILE, TILE)
            body(dn_out, pl.ds(start, TILE), pl.ds(start, TILE))

        def up_tile(i):
            start = pl.multiple_of(i * TILE, TILE)
            body(up_out, pl.ds(start, TILE), pl.ds(pl.multiple_of(model + start, TILE), TILE))

        loop(model // TILE, dn_tile)
        loop(hidden // TILE, up_tile)
        body(rt_out, pl.ds(0, PIECE), pl.ds(both, PIECE))

    def first_terms(out, here, there):
        out[:, here] = part[own, :, there].astype(F32) + x_in[z, :, there].astype(F32)

    def left_term(out, here, there):
        out[:, here] += left_in[z, :, there].astype(F32)

    def right_term(out, here, there):
        out[:, here] += right_in[z, :, there].astype(F32)

    def take_left():
        right_copy(z).wait_recv()
        results(left_term)

    def take_right():
        left_copy(z).wait_recv()
        results(right_term)

    x_copy(z).wait_recv()
    results(first_terms)
    pl.when(z > 0)(take_left)
    pl.when(z < 3)(take_right)

    for zz in range(4):
        pl.when((z < 3) & (zz <= z))(lambda zz=zz: to_right(zz).wait_send())
        pl.when((z > 0) & (zz >= z))(lambda zz=zz: to_left(zz).wait_send())
        to_x(zz).wait_send()
        x_copy(zz).wait_send()
        pl.when(zz > z)(lambda zz=zz: right_copy(zz).wait_send())
        pl.when(zz < z)(lambda zz=zz: left_copy(zz).wait_send())
        for xx in range(2):
            to_core(zz, xx).wait_send()
            y_to_core(zz, xx).wait_send()
            pl.when((zz != z) | (xx != x))(lambda zz=zz, xx=xx: to_y(zz, xx).wait_send())
            core_copy(zz, xx).wait_send()


def fused(tokens, grad_up, tenant_ids, expert_ids, adapter_down, adapter_up, router):
    rows, model = tokens.shape
    hidden = grad_up.shape[1]
    rank = adapter_down.shape[1]
    both = model + hidden
    total = both + PIECE
    ids = tenant_ids[:, None] * EXP_TEN + expert_ids
    vmem = pl.BlockSpec(memory_space=pltpu.VMEM)
    dma = pltpu.SemaphoreType.DMA
    tok_out, dn_out, up_out, rt_out = pl.pallas_call(
        fused_kernel,
        out_shape=(
            jax.ShapeDtypeStruct((rows, model), BF16),
            jax.ShapeDtypeStruct((rank, model), F32),
            jax.ShapeDtypeStruct((rank, hidden), F32),
            jax.ShapeDtypeStruct((16, PIECE), F32),
        ),
        in_specs=[vmem] * 6,
        out_specs=(vmem,) * 4,
        scratch_shapes=[
            pltpu.VMEM((16, rank, both), BF16),
            pltpu.VMEM((16, rank, total), BF16),
            pltpu.VMEM((8, rank, total), BF16),
            pltpu.VMEM((4, rank, total), BF16),
            pltpu.VMEM((4, rank, total), BF16),
            pltpu.VMEM((4, rank, total), BF16),
            pltpu.VMEM((rows, 256), F32),
            pltpu.VMEM((rows, 256), F32),
            pltpu.VMEM((rows, 16), F32),
            pltpu.VMEM((rows, 256), BF16),
            pltpu.VMEM((256, rows), BF16),
            pltpu.VMEM((256, rows), BF16),
            pltpu.VMEM((256, rows), BF16),
            pltpu.VMEM((rows, 16), BF16),
            pltpu.VMEM((128, PIECE), F32),
            dma((3,)), dma((20,)), dma((16,)), dma((16,)), dma((16,)), dma((8,)), dma((8,)),
            dma((4,)), dma((4,)), dma((4,)), dma((4,)), dma((4,)),
        ],
        compiler_params=pltpu.CompilerParams(
            collective_id=0, has_side_effects=True, vmem_limit_bytes=60 * 1024 * 1024
        ),
    )(tokens, grad_up, ids, adapter_down[0], adapter_up[0], router)
    return (tok_out, dn_out[None], up_out[None], rt_out.reshape(1, model))


def per_device(tokens, grad_up, tenant_ids, expert_ids, adapter_down, adapter_up, router):
    planes = lax.axis_size("tenant") == 16 and lax.axis_size("group") == 2
    fits = planes and tokens.shape[0] == 128 and adapter_down.shape[1] == 16
    plan = fused if fits else routed
    return plan(tokens, grad_up, tenant_ids, expert_ids, adapter_down, adapter_up, router)


def solution(mesh):
    in_specs = (
        P(("group", "tenant"), None),
        P(("group", "tenant"), None),
        P(("group", "tenant")),
        P(("group", "tenant"), None),
        P("tenant", None, None),
        P("tenant", None, None),
        P(),
    )
    out_specs = (
        P(("group", "tenant"), None),
        P(("group", "tenant"), None, None),
        P(("group", "tenant"), None, None),
        P(("group", "tenant"), None),
    )
    return jax.shard_map(
        per_device, mesh=mesh, in_specs=in_specs, out_specs=out_specs, check_vma=False
    )
```

```python
import jax
import jax.numpy as jnp
import functools

from jax import lax
from jax.experimental import pallas as pl
from jax.experimental.pallas import tpu as pltpu
from jax.sharding import PartitionSpec as P

EXP_TEN = 8


adapter_scale_factor = 2.0


def routed(tokens, grad_up, tenant_ids, expert_ids, adapter_down, adapter_up, router):
    tok_rows = tokens.shape[0]
    model_width = tokens.shape[1]
    hidden_width = grad_up.shape[1]
    devices = lax.axis_size("tenant")
    capacity = 2 * tok_rows // devices
    buffer_len = devices * capacity
    global_ids = tenant_ids[:, None] * EXP_TEN + expert_ids
    logits = lax.dot_general(
        tokens, router, (((1,), (1,)), ((), ())), preferred_element_type=jnp.float32
    )
    picked = jnp.take_along_axis(logits, global_ids, axis=1)
    first_gate = jax.nn.sigmoid(picked[:, 0] - picked[:, 1])
    gate_sent = jnp.stack([first_gate, 1.0 - first_gate], axis=1).astype(jnp.bfloat16)
    flat_ids = global_ids.reshape(-1)
    slot_count = flat_ids.shape[0]
    same_owner = flat_ids[:, None] == flat_ids[None, :]
    slot_line = jnp.arange(slot_count, dtype=jnp.int32)
    earlier = slot_line[None, :] < slot_line[:, None]
    ranks = jnp.sum((same_owner & earlier).astype(jnp.int32), axis=1)
    places = (flat_ids * capacity + ranks).reshape(tok_rows, 2)

    def spread_rows(values):
        empty = jnp.zeros((buffer_len,) + values.shape[1:], values.dtype)
        return empty.at[places[:, 0]].set(values).at[places[:, 1]].set(values)

    send_rows = spread_rows(tokens).reshape(devices, capacity, model_width)
    send_grads = spread_rows(grad_up).reshape(devices, capacity, hidden_width)
    empty_gates = jnp.zeros((buffer_len,), jnp.bfloat16)
    send_gates = (
        empty_gates.at[places[:, 0]]
        .set(gate_sent[:, 0])
        .at[places[:, 1]]
        .set(gate_sent[:, 1])
        .reshape(devices, capacity)
    )
    recv_rows, recv_grads, recv_gates = (
        lax.all_to_all(send_rows, "tenant", split_axis=0, concat_axis=0, tiled=True),
        lax.all_to_all(send_grads, "tenant", split_axis=0, concat_axis=0, tiled=True),
        lax.all_to_all(send_gates, "tenant", split_axis=0, concat_axis=0, tiled=True),
    )
    rows_in = recv_rows.reshape(buffer_len, model_width)
    grads_in = recv_grads.reshape(buffer_len, hidden_width)
    incoming_gate_values = recv_gates.reshape(buffer_len).astype(jnp.float32)
    down = adapter_down[0]
    upper = adapter_up[0]
    reduced_rank_activations = lax.dot_general(
        rows_in, down, (((1,), (1,)), ((), ())), preferred_element_type=jnp.float32
    )
    returned_rank_gradient = lax.dot_general(
        grads_in, upper, (((1,), (1,)), ((), ())), preferred_element_type=jnp.float32
    )
    position_gate_value = (
        adapter_scale_factor * jnp.sum(reduced_rank_activations * returned_rank_gradient, axis=1)
    ).astype(jnp.bfloat16)
    gate_weighted_output = (
        adapter_scale_factor * incoming_gate_values[:, None] * returned_rank_gradient
    ).astype(jnp.bfloat16)
    scaled_reduced_activations = (
        adapter_scale_factor * incoming_gate_values[:, None] * reduced_rank_activations
    ).astype(jnp.bfloat16)
    slot_rows = jnp.dot(gate_weighted_output, down, preferred_element_type=jnp.float32).astype(
        jnp.bfloat16
    )
    back_rows, back_gates = (
        lax.all_to_all(
            slot_rows.reshape(devices, capacity, model_width),
            "tenant",
            split_axis=0,
            concat_axis=0,
            tiled=True,
        ),
        lax.all_to_all(
            position_gate_value.reshape(devices, capacity),
            "tenant",
            split_axis=0,
            concat_axis=0,
            tiled=True,
        ),
    )
    grad_down = lax.dot_general(
        gate_weighted_output, rows_in, (((0,), (0,)), ((), ())), preferred_element_type=jnp.float32
    )
    grad_upper = lax.dot_general(
        scaled_reduced_activations,
        grads_in,
        (((0,), (0,)), ((), ())),
        preferred_element_type=jnp.float32,
    )
    flat_back = back_rows.reshape(buffer_len, model_width)
    expert_grad = flat_back[places[:, 0]].astype(jnp.float32) + flat_back[places[:, 1]].astype(
        jnp.float32
    )
    gate_grads = back_gates.reshape(buffer_len)[places].astype(jnp.float32)
    logit_grad = first_gate * (1.0 - first_gate) * (gate_grads[:, 0] - gate_grads[:, 1])
    logit_sent = logit_grad.astype(jnp.bfloat16)
    columns = jnp.arange(router.shape[0], dtype=jnp.int32)[None, :]
    nothing = jnp.zeros((), jnp.bfloat16)
    signed = jnp.where(columns == global_ids[:, 0:1], logit_sent[:, None], nothing) - jnp.where(
        columns == global_ids[:, 1:2], logit_sent[:, None], nothing
    )
    router_term = jnp.dot(signed, router, preferred_element_type=jnp.float32)
    token_grad = (expert_grad + router_term).astype(jnp.bfloat16)
    router_grad = lax.psum_scatter(
        lax.dot_general(
            signed, tokens, (((0,), (0,)), ((), ())), preferred_element_type=jnp.float32
        ),
        "tenant",
        scatter_dimension=0,
        tiled=True,
    )
    return (token_grad, grad_down[None], grad_upper[None], router_grad)


F32 = jnp.float32
BF16 = jnp.bfloat16
TILE = 1024
PIECE = 512


def loop(count, body):
    def step(i, carry):
        body(i)
        return carry

    lax.fori_loop(0, count, step, 0)


def fused_kernel(
    tok, gup, ids, adn, aup, router,
    tok_out, dn_out, up_out, rt_out,
    fac, part, core_in, x_in, left_in, right_in,
    low, back, logits, wide, wide_t, scaled_t, sign_t, signed, acc,
    own_sem, ag_send, ag_recv, y_send, y_recv, core_send, core_recv, x_send, x_recv, z_send, left_recv, right_recv,
):
    me = lax.axis_index("tenant")
    g = lax.axis_index("group")
    c = lax.rem(me, 2)
    x = lax.rem(lax.div(me, 2), 2)
    z = lax.div(me, 4)
    model = tok.shape[1]
    hidden = gup.shape[1]
    half = hidden // 2
    both = model + hidden
    total = part.shape[2]
    rows = tok.shape[0]

    right = me + 4
    left = me - 4
    x_peer = me + 2 - 4 * x
    c_peer = me + 1 - 2 * c

    def slot(cc, zz, xx):
        return cc * 8 + zz * 2 + xx

    barrier = pltpu.get_barrier_semaphore()

    def greet(peer, group=g):
        pl.semaphore_signal(
            barrier,
            inc=1,
            device_id={"group": group, "tenant": peer},
            device_id_type=pl.DeviceIdType.MESH,
        )

    own = slot(c, z, x)
    own_dn = pltpu.make_async_copy(adn, fac.at[own, :, pl.ds(half, model)], own_sem.at[0])
    own_lo = pltpu.make_async_copy(
        aup.at[:, pl.ds(0, half)], fac.at[own, :, pl.ds(0, half)], own_sem.at[1]
    )
    own_hi = pltpu.make_async_copy(
        aup.at[:, pl.ds(half, half)], fac.at[own, :, pl.ds(half + model, half)], own_sem.at[2]
    )
    own_dn.start()
    own_lo.start()
    own_hi.start()
    greet(x_peer)
    greet(c_peer)
    greet(me, 1 - g)
    pl.when(z < 3)(lambda: greet(right))
    pl.when(z > 0)(lambda: greet(left))
    pl.semaphore_wait(
        barrier, 3 + jnp.where(z < 3, 1, 0).astype(jnp.int32) + jnp.where(z > 0, 1, 0).astype(jnp.int32)
    )
    own_dn.wait()
    own_lo.wait()
    own_hi.wait()

    def remote(src, dst, send, recv, peer, group=g):
        return pltpu.make_async_remote_copy(
            src_ref=src, dst_ref=dst, send_sem=send, recv_sem=recv,
            device_id={"group": group, "tenant": peer}, device_id_type=pl.DeviceIdType.MESH,
        )

    gathered = pl.ds(pl.multiple_of(g * half, 128), half + model)
    mine_y = pl.ds(pl.multiple_of(g * (half + model), 128), half)
    other_y = pl.ds(pl.multiple_of((1 - g) * (half + model), 128), half)

    def gather_copy(at, send_at, peer):
        block = fac.at[at, :, gathered]
        return remote(block, block, ag_send.at[send_at], ag_recv.at[at], peer)

    def to_y(zz, xx):
        at = slot(c, zz, xx)
        block = fac.at[at, :, mine_y]
        return remote(block, block, y_send.at[zz * 2 + xx], y_recv.at[at], me, 1 - g)

    def y_to_core(zz, xx):
        at = slot(c, zz, xx)
        block = fac.at[at, :, other_y]
        return remote(block, block, y_send.at[8 + zz * 2 + xx], y_recv.at[at], c_peer)

    def y_arrived(at):
        block = fac.at[at, :, other_y]
        remote(block, block, y_send.at[0], y_recv.at[at], c_peer).wait_recv()

    def to_right(zz):
        return gather_copy(slot(c, zz, x), zz, right)

    def to_left(zz):
        return gather_copy(slot(c, zz, x), 4 + zz, left)

    def to_x(zz):
        return gather_copy(slot(c, zz, x), 8 + zz, x_peer)

    def to_core(zz, xx):
        return gather_copy(slot(c, zz, xx), 12 + zz * 2 + xx, c_peer)

    def arrived(at):
        gather_copy(at, 0, c_peer).wait_recv()

    pl.when(z < 3)(lambda: to_right(z).start())
    pl.when(z > 0)(lambda: to_left(z).start())
    to_x(z).start()
    to_core(z, x).start()
    y_to_core(z, x).start()

    nt = (((1,), (1,)), ((), ()))
    logits[...] = jnp.zeros_like(logits)

    def logit_tile(i):
        cols = pl.ds(pl.multiple_of(i * TILE, TILE), TILE)
        logits[...] += lax.dot_general(tok[:, cols], router[:, cols], nt, preferred_element_type=F32)

    loop(model // TILE, logit_tile)

    for s in range(1, 4):
        def from_left(s=s):
            arrived(slot(c, z - s, x))
            pl.when(z < 3)(lambda: to_right(z - s).start())
            to_x(z - s).start()
            to_y(z - s, x).start()
            to_core(z - s, x).start()

        def from_right(s=s):
            arrived(slot(c, z + s, x))
            pl.when(z > 0)(lambda: to_left(z + s).start())
            to_x(z + s).start()
            to_y(z + s, x).start()
            to_core(z + s, x).start()

        pl.when(z - s >= 0)(from_left)
        pl.when(z + s <= 3)(from_right)

    def x_block(zz):
        arrived(slot(c, zz, 1 - x))
        to_y(zz, 1 - x).start()
        to_core(zz, 1 - x).start()

    def y_block(zz, xx):
        y_arrived(slot(c, zz, xx))
        y_to_core(zz, xx).start()

    x_block(z)
    for s in range(1, 4):
        for inside, zz in ((z - s >= 0, z - s), (z + s <= 3, z + s)):
            pl.when(inside)(functools.partial(y_block, zz, x))
            pl.when(inside)(functools.partial(x_block, zz))
    y_block(z, 1 - x)
    for s in range(1, 4):
        for inside, zz in ((z - s >= 0, z - s), (z + s <= 3, z + s)):
            pl.when(inside)(functools.partial(y_block, zz, 1 - x))
    for k in range(8):
        arrived((1 - c) * 8 + k)

    def factor_tile(start):
        return fac[:, :, pl.ds(start, TILE)].reshape(256, TILE)

    low[...] = jnp.zeros_like(low)
    back[...] = jnp.zeros_like(back)

    def low_tile(i):
        start = pl.multiple_of(i * TILE, TILE)
        low[...] += lax.dot_general(
            tok[:, pl.ds(start, TILE)],
            factor_tile(pl.multiple_of(half + start, TILE)),
            nt,
            preferred_element_type=F32
        )

    def back_tile(i):
        start = pl.multiple_of(i * TILE, TILE)
        back[...] += lax.dot_general(
            gup[:, pl.ds(start, TILE)],
            factor_tile(pl.multiple_of(start + jnp.where(start >= half, model, 0), TILE)),
            nt,
            preferred_element_type=F32,
        )

    loop(model // TILE, low_tile)
    for k in range(8):
        y_arrived((1 - c) * 8 + k)
    loop(hidden // TILE, back_tile)

    first = ids[:, 0:1]
    second = ids[:, 1:2]
    narrow = lax.broadcasted_iota(jnp.int32, (rows, 16), 1)
    n_sign = jnp.where(narrow == first, 1.0, 0.0) - jnp.where(narrow == second, 1.0, 0.0)
    first_gate = jax.nn.sigmoid(jnp.sum(logits[...] * n_sign, axis=1, keepdims=True))
    place = lax.broadcasted_iota(jnp.int32, (rows, 256), 1) // 16
    expert = (place % 8) * 2 + place // 8
    hot1 = expert == first
    hot2 = expert == second
    one = first_gate.astype(BF16).astype(F32)
    two = (1.0 - first_gate).astype(BF16).astype(F32)
    gates = adapter_scale_factor * (jnp.where(hot1, one, 0.0) + jnp.where(hot2, two, 0.0))
    lows = low[...]
    backs = back[...]
    weighted = gates * backs
    product = lows * backs

    def slot_gate(hot):
        picked = jnp.sum(jnp.where(hot, product, 0.0), axis=1, keepdims=True)
        return (adapter_scale_factor * picked).astype(BF16).astype(F32)

    logit_sent = first_gate * (1.0 - first_gate) * (slot_gate(hot1) - slot_gate(hot2))
    signed[...] = (logit_sent * n_sign).astype(BF16)
    w_sign = jnp.where(hot1, logit_sent, 0.0) - jnp.where(hot2, logit_sent, 0.0)
    wide[...] = weighted.astype(BF16)
    wide_t[...] = weighted.T.astype(BF16)
    scaled_t[...] = (gates * lows).T.astype(BF16)
    sign_t[...] = w_sign.T.astype(BF16)

    chunks = ((0, model), (model, half), (model + half, half + PIECE))

    def dn_products():
        def tile(i):
            cols = pl.ds(pl.multiple_of(i * PIECE, PIECE), PIECE)
            made = jnp.dot(wide_t[...], tok[:, cols], preferred_element_type=F32)
            part[:, :, cols] = made.astype(BF16).reshape(16, 16, PIECE)

        loop(model // PIECE, tile)

    def up_products(start):
        def tile(i):
            at = pl.multiple_of(start + i * PIECE, PIECE)
            made = jnp.dot(scaled_t[...], gup[:, pl.ds(at, PIECE)], preferred_element_type=F32)
            part[:, :, pl.ds(pl.multiple_of(model + at, PIECE), PIECE)] = made.astype(BF16).reshape(
                16, 16, PIECE
            )

        loop(half // PIECE, tile)

    def router_products():
        acc[...] = jnp.zeros_like(acc)
        line = lax.broadcasted_iota(jnp.int32, (256, PIECE), 0) % 16

        def tile(i):
            cols = pl.ds(pl.multiple_of(i * PIECE, PIECE), PIECE)
            made = jnp.dot(sign_t[...], tok[:, cols], preferred_element_type=F32)
            acc[...] = jnp.where(line == i, made, acc[...])

        loop(16, tile)
        part[:, :, pl.ds(both, PIECE)] = acc[...].astype(BF16).reshape(16, 16, PIECE)

    def order(k):
        low_half = (3, 2, 1 - z, z)[k]
        high_half = (0, 1, 5 - z, z)[k]
        return jnp.where(z < 2, low_half, high_half)

    def reduce_copy(q, source, target, to, send, recv, sem_at, peer):
        cols = pl.ds(*chunks[q])
        return remote(
            part.at[source, :, cols], target.at[to, :, cols],
            send.at[q, sem_at], recv.at[q, sem_at], peer,
        )

    def core_copy(q, zz, xx):
        at = zz * 2 + xx
        return reduce_copy(
            q, slot(1 - c, zz, xx), core_in, at, core_send, core_recv, at, c_peer
        )

    def x_copy(q, zz):
        return reduce_copy(q, slot(c, zz, 1 - x), x_in, zz, x_send, x_recv, zz, x_peer)

    def right_copy(q, zz):
        return reduce_copy(q, slot(c, zz, x), left_in, zz, z_send, left_recv, zz, right)

    def left_copy(q, zz):
        return reduce_copy(q, slot(c, zz, x), right_in, zz, z_send, right_recv, zz, left)

    def add(q, at, buf, index):
        begin, size = chunks[q]

        def add_cols(cols):
            part[at, :, cols] = (
                part[at, :, cols].astype(F32) + buf[index, :, cols].astype(F32)
            ).astype(BF16)

        loop(size // 2048, lambda i: add_cols(pl.ds(pl.multiple_of(begin + i * 2048, PIECE), 2048)))
        if size % 2048:
            add_cols(pl.ds(begin + size // 2048 * 2048, size % 2048))

    def to_core_peer(q):
        for k in range(4):
            core_copy(q, order(k), 1 - x).start()
        for k in range(4):
            core_copy(q, order(k), x).start()

    def x_stage(q):
        for k in range(4):
            d = order(k)
            core_copy(q, d, 1 - x).wait_recv()
            add(q, slot(c, d, 1 - x), core_in, d * 2 + 1 - x)
            x_copy(q, d).start()

    def own_stage(q):
        for k in range(4):
            d = order(k)
            core_copy(q, d, x).wait_recv()
            add(q, slot(c, d, x), core_in, d * 2 + x)

    dn_products()
    to_core_peer(0)
    up_products(0)
    to_core_peer(1)
    x_stage(0)
    up_products(half)
    router_products()
    to_core_peer(2)
    x_stage(1)
    own_stage(0)
    x_stage(2)

    def token_tile(i):
        start = pl.multiple_of(i * TILE, TILE)
        cols = pl.ds(start, TILE)
        tok_out[:, cols] = (
            jnp.dot(
                wide[...], factor_tile(pl.multiple_of(half + start, TILE)), preferred_element_type=F32
            )
            + jnp.dot(signed[...], router[:, cols], preferred_element_type=F32)
        ).astype(BF16)

    def z_stage(q):
        for k in range(3):
            d = order(k)
            mine = slot(c, d, x)
            x_copy(q, d).wait_recv()
            add(q, mine, x_in, d)

            def rightward(d=d, mine=mine):
                def more():
                    right_copy(q, d).wait_recv()
                    add(q, mine, left_in, d)

                pl.when(z > 0)(more)
                right_copy(q, d).start()

            def leftward(d=d, mine=mine):
                def more():
                    left_copy(q, d).wait_recv()
                    add(q, mine, right_in, d)

                pl.when(z < 3)(more)
                left_copy(q, d).start()

            pl.when(d > z)(rightward)
            pl.when(d < z)(leftward)

    z_stage(0)
    own_stage(1)
    own_stage(2)
    loop(model // TILE, token_tile)
    z_stage(1)
    z_stage(2)

    def results(body):
        def dn_tile(i):
            start = pl.multiple_of(i * TILE, TILE)
            body(dn_out, pl.ds(start, TILE), pl.ds(start, TILE))

        def up_tile(i):
            start = pl.multiple_of(i * TILE, TILE)
            body(up_out, pl.ds(start, TILE), pl.ds(pl.multiple_of(model + start, TILE), TILE))

        loop(model // TILE, dn_tile)
        loop(hidden // TILE, up_tile)
        body(rt_out, pl.ds(0, PIECE), pl.ds(both, PIECE))

    def first_terms(out, here, there):
        out[:, here] = part[own, :, there].astype(F32) + x_in[z, :, there].astype(F32)

    def left_term(out, here, there):
        out[:, here] += left_in[z, :, there].astype(F32)

    def right_term(out, here, there):
        out[:, here] += right_in[z, :, there].astype(F32)

    def take_left():
        for q in range(3):
            right_copy(q, z).wait_recv()
        results(left_term)

    def take_right():
        for q in range(3):
            left_copy(q, z).wait_recv()
        results(right_term)

    for q in range(3):
        x_copy(q, z).wait_recv()
    results(first_terms)
    pl.when(z > 0)(take_left)
    pl.when(z < 3)(take_right)

    for zz in range(4):
        pl.when((z < 3) & (zz <= z))(lambda zz=zz: to_right(zz).wait_send())
        pl.when((z > 0) & (zz >= z))(lambda zz=zz: to_left(zz).wait_send())
        to_x(zz).wait_send()
        for q in range(3):
            x_copy(q, zz).wait_send()
            pl.when(zz > z)(lambda q=q, zz=zz: right_copy(q, zz).wait_send())
            pl.when(zz < z)(lambda q=q, zz=zz: left_copy(q, zz).wait_send())
        for xx in range(2):
            to_core(zz, xx).wait_send()
            y_to_core(zz, xx).wait_send()
            pl.when((zz != z) | (xx != x))(lambda zz=zz, xx=xx: to_y(zz, xx).wait_send())
            for q in range(3):
                core_copy(q, zz, xx).wait_send()


def fused(tokens, grad_up, tenant_ids, expert_ids, adapter_down, adapter_up, router):
    rows, model = tokens.shape
    hidden = grad_up.shape[1]
    rank = adapter_down.shape[1]
    both = model + hidden
    total = both + PIECE
    ids = tenant_ids[:, None] * EXP_TEN + expert_ids
    vmem = pl.BlockSpec(memory_space=pltpu.VMEM)
    dma = pltpu.SemaphoreType.DMA
    tok_out, dn_out, up_out, rt_out = pl.pallas_call(
        fused_kernel,
        out_shape=(
            jax.ShapeDtypeStruct((rows, model), BF16),
            jax.ShapeDtypeStruct((rank, model), F32),
            jax.ShapeDtypeStruct((rank, hidden), F32),
            jax.ShapeDtypeStruct((16, PIECE), F32),
        ),
        in_specs=[vmem] * 6,
        out_specs=(vmem,) * 4,
        scratch_shapes=[
            pltpu.VMEM((16, rank, both), BF16),
            pltpu.VMEM((16, rank, total), BF16),
            pltpu.VMEM((8, rank, total), BF16),
            pltpu.VMEM((4, rank, total), BF16),
            pltpu.VMEM((4, rank, total), BF16),
            pltpu.VMEM((4, rank, total), BF16),
            pltpu.VMEM((rows, 256), F32),
            pltpu.VMEM((rows, 256), F32),
            pltpu.VMEM((rows, 16), F32),
            pltpu.VMEM((rows, 256), BF16),
            pltpu.VMEM((256, rows), BF16),
            pltpu.VMEM((256, rows), BF16),
            pltpu.VMEM((256, rows), BF16),
            pltpu.VMEM((rows, 16), BF16),
            pltpu.VMEM((256, PIECE), F32),
            dma((3,)), dma((20,)), dma((16,)), dma((16,)), dma((16,)), dma((3, 8)), dma((3, 8)),
            dma((3, 4)), dma((3, 4)), dma((3, 4)), dma((3, 4)), dma((3, 4)),
        ],
        compiler_params=pltpu.CompilerParams(
            collective_id=0, has_side_effects=True, vmem_limit_bytes=60 * 1024 * 1024
        ),
    )(tokens, grad_up, ids, adapter_down[0], adapter_up[0], router)
    return (tok_out, dn_out[None], up_out[None], rt_out.reshape(1, model))


def per_device(tokens, grad_up, tenant_ids, expert_ids, adapter_down, adapter_up, router):
    planes = lax.axis_size("tenant") == 16 and lax.axis_size("group") == 2
    fits = planes and tokens.shape[0] == 128 and adapter_down.shape[1] == 16
    plan = fused if fits else routed
    return plan(tokens, grad_up, tenant_ids, expert_ids, adapter_down, adapter_up, router)


def solution(mesh):
    in_specs = (
        P(("group", "tenant"), None),
        P(("group", "tenant"), None),
        P(("group", "tenant")),
        P(("group", "tenant"), None),
        P("tenant", None, None),
        P("tenant", None, None),
        P(),
    )
    out_specs = (
        P(("group", "tenant"), None),
        P(("group", "tenant"), None, None),
        P(("group", "tenant"), None, None),
        P(("group", "tenant"), None),
    )
    return jax.shard_map(
        per_device, mesh=mesh, in_specs=in_specs, out_specs=out_specs, check_vma=False
    )
```

```python
import jax
import jax.numpy as jnp
import functools

from jax import lax
from jax.experimental import pallas as pl
from jax.experimental.pallas import tpu as pltpu
from jax.sharding import PartitionSpec as P

EXP_TEN = 8


adapter_scale_factor = 2.0


def routed(tokens, grad_up, tenant_ids, expert_ids, adapter_down, adapter_up, router):
    tok_rows = tokens.shape[0]
    model_width = tokens.shape[1]
    hidden_width = grad_up.shape[1]
    devices = lax.axis_size("tenant")
    capacity = 2 * tok_rows // devices
    buffer_len = devices * capacity
    global_ids = tenant_ids[:, None] * EXP_TEN + expert_ids
    logits = lax.dot_general(
        tokens, router, (((1,), (1,)), ((), ())), preferred_element_type=jnp.float32
    )
    picked = jnp.take_along_axis(logits, global_ids, axis=1)
    first_gate = jax.nn.sigmoid(picked[:, 0] - picked[:, 1])
    gate_sent = jnp.stack([first_gate, 1.0 - first_gate], axis=1).astype(jnp.bfloat16)
    flat_ids = global_ids.reshape(-1)
    slot_count = flat_ids.shape[0]
    same_owner = flat_ids[:, None] == flat_ids[None, :]
    slot_line = jnp.arange(slot_count, dtype=jnp.int32)
    earlier = slot_line[None, :] < slot_line[:, None]
    ranks = jnp.sum((same_owner & earlier).astype(jnp.int32), axis=1)
    places = (flat_ids * capacity + ranks).reshape(tok_rows, 2)

    def spread_rows(values):
        empty = jnp.zeros((buffer_len,) + values.shape[1:], values.dtype)
        return empty.at[places[:, 0]].set(values).at[places[:, 1]].set(values)

    send_rows = spread_rows(tokens).reshape(devices, capacity, model_width)
    send_grads = spread_rows(grad_up).reshape(devices, capacity, hidden_width)
    empty_gates = jnp.zeros((buffer_len,), jnp.bfloat16)
    send_gates = (
        empty_gates.at[places[:, 0]]
        .set(gate_sent[:, 0])
        .at[places[:, 1]]
        .set(gate_sent[:, 1])
        .reshape(devices, capacity)
    )
    recv_rows, recv_grads, recv_gates = (
        lax.all_to_all(send_rows, "tenant", split_axis=0, concat_axis=0, tiled=True),
        lax.all_to_all(send_grads, "tenant", split_axis=0, concat_axis=0, tiled=True),
        lax.all_to_all(send_gates, "tenant", split_axis=0, concat_axis=0, tiled=True),
    )
    rows_in = recv_rows.reshape(buffer_len, model_width)
    grads_in = recv_grads.reshape(buffer_len, hidden_width)
    incoming_gate_values = recv_gates.reshape(buffer_len).astype(jnp.float32)
    down = adapter_down[0]
    upper = adapter_up[0]
    reduced_rank_activations = lax.dot_general(
        rows_in, down, (((1,), (1,)), ((), ())), preferred_element_type=jnp.float32
    )
    returned_rank_gradient = lax.dot_general(
        grads_in, upper, (((1,), (1,)), ((), ())), preferred_element_type=jnp.float32
    )
    position_gate_value = (
        adapter_scale_factor * jnp.sum(reduced_rank_activations * returned_rank_gradient, axis=1)
    ).astype(jnp.bfloat16)
    gate_weighted_output = (
        adapter_scale_factor * incoming_gate_values[:, None] * returned_rank_gradient
    ).astype(jnp.bfloat16)
    scaled_reduced_activations = (
        adapter_scale_factor * incoming_gate_values[:, None] * reduced_rank_activations
    ).astype(jnp.bfloat16)
    slot_rows = jnp.dot(gate_weighted_output, down, preferred_element_type=jnp.float32).astype(
        jnp.bfloat16
    )
    back_rows, back_gates = (
        lax.all_to_all(
            slot_rows.reshape(devices, capacity, model_width),
            "tenant",
            split_axis=0,
            concat_axis=0,
            tiled=True,
        ),
        lax.all_to_all(
            position_gate_value.reshape(devices, capacity),
            "tenant",
            split_axis=0,
            concat_axis=0,
            tiled=True,
        ),
    )
    grad_down = lax.dot_general(
        gate_weighted_output, rows_in, (((0,), (0,)), ((), ())), preferred_element_type=jnp.float32
    )
    grad_upper = lax.dot_general(
        scaled_reduced_activations,
        grads_in,
        (((0,), (0,)), ((), ())),
        preferred_element_type=jnp.float32,
    )
    flat_back = back_rows.reshape(buffer_len, model_width)
    expert_grad = flat_back[places[:, 0]].astype(jnp.float32) + flat_back[places[:, 1]].astype(
        jnp.float32
    )
    gate_grads = back_gates.reshape(buffer_len)[places].astype(jnp.float32)
    logit_grad = first_gate * (1.0 - first_gate) * (gate_grads[:, 0] - gate_grads[:, 1])
    logit_sent = logit_grad.astype(jnp.bfloat16)
    columns = jnp.arange(router.shape[0], dtype=jnp.int32)[None, :]
    nothing = jnp.zeros((), jnp.bfloat16)
    signed = jnp.where(columns == global_ids[:, 0:1], logit_sent[:, None], nothing) - jnp.where(
        columns == global_ids[:, 1:2], logit_sent[:, None], nothing
    )
    router_term = jnp.dot(signed, router, preferred_element_type=jnp.float32)
    token_grad = (expert_grad + router_term).astype(jnp.bfloat16)
    router_grad = lax.psum_scatter(
        lax.dot_general(
            signed, tokens, (((0,), (0,)), ((), ())), preferred_element_type=jnp.float32
        ),
        "tenant",
        scatter_dimension=0,
        tiled=True,
    )
    return (token_grad, grad_down[None], grad_upper[None], router_grad)


F32 = jnp.float32
BF16 = jnp.bfloat16
TILE = 1024
PIECE = 512


def loop(count, body):
    def step(i, carry):
        body(i)
        return carry

    lax.fori_loop(0, count, step, 0)


def fused_kernel(
    tok_in, gup_in, ids, adn, aup, router,
    tok_out, dn_out, up_out, rt_out,
    tok, gup, fac, part, core_in, x_in, left_in, right_in,
    low, back, logits, wide, wide_t, scaled_t, sign_t, signed, acc,
    own_sem, ag_send, ag_recv, y_send, y_recv, core_send, core_recv, x_send, x_recv, z_send, left_recv, right_recv,
):
    me = lax.axis_index("tenant")
    g = lax.axis_index("group")
    c = lax.rem(me, 2)
    x = lax.rem(lax.div(me, 2), 2)
    z = lax.div(me, 4)
    model = tok.shape[1]
    hidden = gup.shape[1]
    half = hidden // 2
    both = model + hidden
    total = part.shape[2]
    rows = tok.shape[0]

    right = me + 4
    left = me - 4
    x_peer = me + 2 - 4 * x
    c_peer = me + 1 - 2 * c

    def slot(cc, zz, xx):
        return cc * 8 + zz * 2 + xx

    barrier = pltpu.get_barrier_semaphore()

    def greet(peer, group=g):
        pl.semaphore_signal(
            barrier,
            inc=1,
            device_id={"group": group, "tenant": peer},
            device_id_type=pl.DeviceIdType.MESH,
        )

    own = slot(c, z, x)
    own_dn = pltpu.make_async_copy(adn, fac.at[own, :, pl.ds(half, model)], own_sem.at[0])
    own_lo = pltpu.make_async_copy(
        aup.at[:, pl.ds(0, half)], fac.at[own, :, pl.ds(0, half)], own_sem.at[1]
    )
    own_hi = pltpu.make_async_copy(
        aup.at[:, pl.ds(half, half)], fac.at[own, :, pl.ds(half + model, half)], own_sem.at[2]
    )
    own_dn.start()
    own_lo.start()
    own_hi.start()
    load_tok = pltpu.make_async_copy(tok_in, tok, own_sem.at[3])
    load_gup = pltpu.make_async_copy(gup_in, gup, own_sem.at[4])
    load_tok.start()
    load_gup.start()
    greet(x_peer)
    greet(c_peer)
    greet(me, 1 - g)
    pl.when(z < 3)(lambda: greet(right))
    pl.when(z > 0)(lambda: greet(left))
    pl.semaphore_wait(
        barrier, 3 + jnp.where(z < 3, 1, 0).astype(jnp.int32) + jnp.where(z > 0, 1, 0).astype(jnp.int32)
    )
    own_dn.wait()
    own_lo.wait()
    own_hi.wait()

    def remote(src, dst, send, recv, peer, group=g):
        return pltpu.make_async_remote_copy(
            src_ref=src, dst_ref=dst, send_sem=send, recv_sem=recv,
            device_id={"group": group, "tenant": peer}, device_id_type=pl.DeviceIdType.MESH,
        )

    gathered = pl.ds(pl.multiple_of(g * half, 128), half + model)
    mine_y = pl.ds(pl.multiple_of(g * (half + model), 128), half)
    other_y = pl.ds(pl.multiple_of((1 - g) * (half + model), 128), half)

    def gather_copy(at, send_at, peer):
        block = fac.at[at, :, gathered]
        return remote(block, block, ag_send.at[send_at], ag_recv.at[at], peer)

    def to_y(zz, xx):
        at = slot(c, zz, xx)
        block = fac.at[at, :, mine_y]
        return remote(block, block, y_send.at[zz * 2 + xx], y_recv.at[at], me, 1 - g)

    def y_to_core(zz, xx):
        at = slot(c, zz, xx)
        block = fac.at[at, :, other_y]
        return remote(block, block, y_send.at[8 + zz * 2 + xx], y_recv.at[at], c_peer)

    def y_arrived(at):
        block = fac.at[at, :, other_y]
        remote(block, block, y_send.at[0], y_recv.at[at], c_peer).wait_recv()

    def to_right(zz):
        return gather_copy(slot(c, zz, x), zz, right)

    def to_left(zz):
        return gather_copy(slot(c, zz, x), 4 + zz, left)

    def to_x(zz):
        return gather_copy(slot(c, zz, x), 8 + zz, x_peer)

    def to_core(zz, xx):
        return gather_copy(slot(c, zz, xx), 12 + zz * 2 + xx, c_peer)

    def arrived(at):
        gather_copy(at, 0, c_peer).wait_recv()

    pl.when(z < 3)(lambda: to_right(z).start())
    pl.when(z > 0)(lambda: to_left(z).start())
    to_x(z).start()
    to_core(z, x).start()
    y_to_core(z, x).start()

    nt = (((1,), (1,)), ((), ()))
    logits[...] = jnp.zeros_like(logits)

    def logit_tile(i):
        cols = pl.ds(pl.multiple_of(i * TILE, TILE), TILE)
        logits[...] += lax.dot_general(tok[:, cols], router[:, cols], nt, preferred_element_type=F32)

    load_tok.wait()
    loop(model // TILE, logit_tile)

    for s in range(1, 4):
        def from_left(s=s):
            arrived(slot(c, z - s, x))
            pl.when(z < 3)(lambda: to_right(z - s).start())
            to_x(z - s).start()
            to_y(z - s, x).start()
            to_core(z - s, x).start()

        def from_right(s=s):
            arrived(slot(c, z + s, x))
            pl.when(z > 0)(lambda: to_left(z + s).start())
            to_x(z + s).start()
            to_y(z + s, x).start()
            to_core(z + s, x).start()

        pl.when(z - s >= 0)(from_left)
        pl.when(z + s <= 3)(from_right)

    def x_block(zz):
        arrived(slot(c, zz, 1 - x))
        to_y(zz, 1 - x).start()
        to_core(zz, 1 - x).start()

    def y_block(zz, xx):
        y_arrived(slot(c, zz, xx))
        y_to_core(zz, xx).start()

    x_block(z)
    for s in range(1, 4):
        for inside, zz in ((z - s >= 0, z - s), (z + s <= 3, z + s)):
            pl.when(inside)(functools.partial(y_block, zz, x))
            pl.when(inside)(functools.partial(x_block, zz))
    y_block(z, 1 - x)
    for s in range(1, 4):
        for inside, zz in ((z - s >= 0, z - s), (z + s <= 3, z + s)):
            pl.when(inside)(functools.partial(y_block, zz, 1 - x))
    for k in range(8):
        arrived((1 - c) * 8 + k)

    def factor_tile(start):
        return fac[:, :, pl.ds(start, TILE)].reshape(256, TILE)

    low[...] = jnp.zeros_like(low)
    back[...] = jnp.zeros_like(back)

    def low_tile(i):
        start = pl.multiple_of(i * TILE, TILE)
        low[...] += lax.dot_general(
            tok[:, pl.ds(start, TILE)],
            factor_tile(pl.multiple_of(half + start, TILE)),
            nt,
            preferred_element_type=F32
        )

    def back_tile(i):
        start = pl.multiple_of(i * TILE, TILE)
        back[...] += lax.dot_general(
            gup[:, pl.ds(start, TILE)],
            factor_tile(pl.multiple_of(start + jnp.where(start >= half, model, 0), TILE)),
            nt,
            preferred_element_type=F32,
        )

    loop(model // TILE, low_tile)
    load_gup.wait()
    per_half = half // TILE
    loop(per_half, lambda i: back_tile(i + g * per_half))
    for k in range(8):
        y_arrived((1 - c) * 8 + k)
    loop(per_half, lambda i: back_tile(i + (1 - g) * per_half))

    first = ids[:, 0:1]
    second = ids[:, 1:2]
    narrow = lax.broadcasted_iota(jnp.int32, (rows, 16), 1)
    n_sign = jnp.where(narrow == first, 1.0, 0.0) - jnp.where(narrow == second, 1.0, 0.0)
    first_gate = jax.nn.sigmoid(jnp.sum(logits[...] * n_sign, axis=1, keepdims=True))
    place = lax.broadcasted_iota(jnp.int32, (rows, 256), 1) // 16
    expert = (place % 8) * 2 + place // 8
    hot1 = expert == first
    hot2 = expert == second
    one = first_gate.astype(BF16).astype(F32)
    two = (1.0 - first_gate).astype(BF16).astype(F32)
    gates = adapter_scale_factor * (jnp.where(hot1, one, 0.0) + jnp.where(hot2, two, 0.0))
    lows = low[...]
    backs = back[...]
    weighted = gates * backs
    product = lows * backs

    def slot_gate(hot):
        picked = jnp.sum(jnp.where(hot, product, 0.0), axis=1, keepdims=True)
        return (adapter_scale_factor * picked).astype(BF16).astype(F32)

    logit_sent = first_gate * (1.0 - first_gate) * (slot_gate(hot1) - slot_gate(hot2))
    signed[...] = (logit_sent * n_sign).astype(BF16)
    w_sign = jnp.where(hot1, logit_sent, 0.0) - jnp.where(hot2, logit_sent, 0.0)
    wide[...] = weighted.astype(BF16)
    wide_t[...] = weighted.T.astype(BF16)
    scaled_t[...] = (gates * lows).T.astype(BF16)
    sign_t[...] = w_sign.T.astype(BF16)

    chunks = ((0, model), (model, half), (model + half, half + PIECE))

    def dn_products():
        def tile(i):
            cols = pl.ds(pl.multiple_of(i * PIECE, PIECE), PIECE)
            made = jnp.dot(wide_t[...], tok[:, cols], preferred_element_type=F32)
            part[:, :, cols] = made.astype(BF16).reshape(16, 16, PIECE)

        loop(model // PIECE, tile)

    def up_products(start):
        def tile(i):
            at = pl.multiple_of(start + i * PIECE, PIECE)
            made = jnp.dot(scaled_t[...], gup[:, pl.ds(at, PIECE)], preferred_element_type=F32)
            part[:, :, pl.ds(pl.multiple_of(model + at, PIECE), PIECE)] = made.astype(BF16).reshape(
                16, 16, PIECE
            )

        loop(half // PIECE, tile)

    def router_products():
        acc[...] = jnp.zeros_like(acc)
        line = lax.broadcasted_iota(jnp.int32, (256, PIECE), 0) % 16

        def tile(i):
            cols = pl.ds(pl.multiple_of(i * PIECE, PIECE), PIECE)
            made = jnp.dot(sign_t[...], tok[:, cols], preferred_element_type=F32)
            acc[...] = jnp.where(line == i, made, acc[...])

        loop(16, tile)
        part[:, :, pl.ds(both, PIECE)] = acc[...].astype(BF16).reshape(16, 16, PIECE)

    def order(k):
        low_half = (3, 2, 1 - z, z)[k]
        high_half = (0, 1, 5 - z, z)[k]
        return jnp.where(z < 2, low_half, high_half)

    def reduce_copy(q, source, target, to, send, recv, sem_at, peer):
        cols = pl.ds(*chunks[q])
        return remote(
            part.at[source, :, cols], target.at[to, :, cols],
            send.at[q, sem_at], recv.at[q, sem_at], peer,
        )

    def core_copy(q, zz, xx):
        at = zz * 2 + xx
        return reduce_copy(
            q, slot(1 - c, zz, xx), core_in, at, core_send, core_recv, at, c_peer
        )

    def x_copy(q, zz):
        return reduce_copy(q, slot(c, zz, 1 - x), x_in, zz, x_send, x_recv, zz, x_peer)

    def right_copy(q, zz):
        return reduce_copy(q, slot(c, zz, x), left_in, zz, z_send, left_recv, zz, right)

    def left_copy(q, zz):
        return reduce_copy(q, slot(c, zz, x), right_in, zz, z_send, right_recv, zz, left)

    def add(q, at, buf, index):
        begin, size = chunks[q]

        def add_cols(cols):
            part[at, :, cols] = (
                part[at, :, cols].astype(F32) + buf[index, :, cols].astype(F32)
            ).astype(BF16)

        loop(size // 2048, lambda i: add_cols(pl.ds(pl.multiple_of(begin + i * 2048, PIECE), 2048)))
        if size % 2048:
            add_cols(pl.ds(begin + size // 2048 * 2048, size % 2048))

    def to_core_peer(q):
        for k in range(4):
            core_copy(q, order(k), 1 - x).start()
        for k in range(4):
            core_copy(q, order(k), x).start()

    def x_stage(q):
        for k in range(4):
            d = order(k)
            core_copy(q, d, 1 - x).wait_recv()
            add(q, slot(c, d, 1 - x), core_in, d * 2 + 1 - x)
            x_copy(q, d).start()

    def own_stage(q):
        for k in range(4):
            d = order(k)
            core_copy(q, d, x).wait_recv()
            add(q, slot(c, d, x), core_in, d * 2 + x)

    dn_products()
    to_core_peer(0)
    up_products(0)
    to_core_peer(1)
    x_stage(0)
    up_products(half)
    router_products()
    to_core_peer(2)
    x_stage(1)
    own_stage(0)
    x_stage(2)

    def token_tile(i):
        start = pl.multiple_of(i * TILE, TILE)
        cols = pl.ds(start, TILE)
        tok_out[:, cols] = (
            jnp.dot(
                wide[...], factor_tile(pl.multiple_of(half + start, TILE)), preferred_element_type=F32
            )
            + jnp.dot(signed[...], router[:, cols], preferred_element_type=F32)
        ).astype(BF16)

    def z_stage(q):
        for k in range(3):
            d = order(k)
            mine = slot(c, d, x)
            x_copy(q, d).wait_recv()
            add(q, mine, x_in, d)

            def rightward(d=d, mine=mine):
                def more():
                    right_copy(q, d).wait_recv()
                    add(q, mine, left_in, d)

                pl.when(z > 0)(more)
                right_copy(q, d).start()

            def leftward(d=d, mine=mine):
                def more():
                    left_copy(q, d).wait_recv()
                    add(q, mine, right_in, d)

                pl.when(z < 3)(more)
                left_copy(q, d).start()

            pl.when(d > z)(rightward)
            pl.when(d < z)(leftward)

    z_stage(0)
    own_stage(1)
    own_stage(2)
    loop(model // TILE, token_tile)
    z_stage(1)
    z_stage(2)

    def results(body):
        def dn_tile(i):
            start = pl.multiple_of(i * TILE, TILE)
            body(dn_out, pl.ds(start, TILE), pl.ds(start, TILE))

        def up_tile(i):
            start = pl.multiple_of(i * TILE, TILE)
            body(up_out, pl.ds(start, TILE), pl.ds(pl.multiple_of(model + start, TILE), TILE))

        loop(model // TILE, dn_tile)
        loop(hidden // TILE, up_tile)
        body(rt_out, pl.ds(0, PIECE), pl.ds(both, PIECE))

    def first_terms(out, here, there):
        out[:, here] = part[own, :, there].astype(F32) + x_in[z, :, there].astype(F32)

    def left_term(out, here, there):
        out[:, here] += left_in[z, :, there].astype(F32)

    def right_term(out, here, there):
        out[:, here] += right_in[z, :, there].astype(F32)

    def take_left():
        for q in range(3):
            right_copy(q, z).wait_recv()
        results(left_term)

    def take_right():
        for q in range(3):
            left_copy(q, z).wait_recv()
        results(right_term)

    for q in range(3):
        x_copy(q, z).wait_recv()
    results(first_terms)
    pl.when(z > 0)(take_left)
    pl.when(z < 3)(take_right)

    for zz in range(4):
        pl.when((z < 3) & (zz <= z))(lambda zz=zz: to_right(zz).wait_send())
        pl.when((z > 0) & (zz >= z))(lambda zz=zz: to_left(zz).wait_send())
        to_x(zz).wait_send()
        for q in range(3):
            x_copy(q, zz).wait_send()
            pl.when(zz > z)(lambda q=q, zz=zz: right_copy(q, zz).wait_send())
            pl.when(zz < z)(lambda q=q, zz=zz: left_copy(q, zz).wait_send())
        for xx in range(2):
            to_core(zz, xx).wait_send()
            y_to_core(zz, xx).wait_send()
            pl.when((zz != z) | (xx != x))(lambda zz=zz, xx=xx: to_y(zz, xx).wait_send())
            for q in range(3):
                core_copy(q, zz, xx).wait_send()


def fused(tokens, grad_up, tenant_ids, expert_ids, adapter_down, adapter_up, router):
    rows, model = tokens.shape
    hidden = grad_up.shape[1]
    rank = adapter_down.shape[1]
    both = model + hidden
    total = both + PIECE
    ids = tenant_ids[:, None] * EXP_TEN + expert_ids
    vmem = pl.BlockSpec(memory_space=pltpu.VMEM)
    hbm = pl.BlockSpec(memory_space=pl.ANY)
    dma = pltpu.SemaphoreType.DMA
    tok_out, dn_out, up_out, rt_out = pl.pallas_call(
        fused_kernel,
        out_shape=(
            jax.ShapeDtypeStruct((rows, model), BF16),
            jax.ShapeDtypeStruct((rank, model), F32),
            jax.ShapeDtypeStruct((rank, hidden), F32),
            jax.ShapeDtypeStruct((16, PIECE), F32),
        ),
        in_specs=[hbm, hbm, vmem, hbm, hbm, vmem],
        out_specs=(vmem,) * 4,
        scratch_shapes=[
            pltpu.VMEM((rows, model), BF16),
            pltpu.VMEM((rows, hidden), BF16),
            pltpu.VMEM((16, rank, both), BF16),
            pltpu.VMEM((16, rank, total), BF16),
            pltpu.VMEM((8, rank, total), BF16),
            pltpu.VMEM((4, rank, total), BF16),
            pltpu.VMEM((4, rank, total), BF16),
            pltpu.VMEM((4, rank, total), BF16),
            pltpu.VMEM((rows, 256), F32),
            pltpu.VMEM((rows, 256), F32),
            pltpu.VMEM((rows, 16), F32),
            pltpu.VMEM((rows, 256), BF16),
            pltpu.VMEM((256, rows), BF16),
            pltpu.VMEM((256, rows), BF16),
            pltpu.VMEM((256, rows), BF16),
            pltpu.VMEM((rows, 16), BF16),
            pltpu.VMEM((256, PIECE), F32),
            dma((5,)), dma((20,)), dma((16,)), dma((16,)), dma((16,)), dma((3, 8)), dma((3, 8)),
            dma((3, 4)), dma((3, 4)), dma((3, 4)), dma((3, 4)), dma((3, 4)),
        ],
        compiler_params=pltpu.CompilerParams(
            collective_id=0, has_side_effects=True, vmem_limit_bytes=60 * 1024 * 1024
        ),
    )(tokens, grad_up, ids, adapter_down[0], adapter_up[0], router)
    return (tok_out, dn_out[None], up_out[None], rt_out.reshape(1, model))


def per_device(tokens, grad_up, tenant_ids, expert_ids, adapter_down, adapter_up, router):
    planes = lax.axis_size("tenant") == 16 and lax.axis_size("group") == 2
    fits = planes and tokens.shape[0] == 128 and adapter_down.shape[1] == 16
    plan = fused if fits else routed
    return plan(tokens, grad_up, tenant_ids, expert_ids, adapter_down, adapter_up, router)


def solution(mesh):
    in_specs = (
        P(("group", "tenant"), None),
        P(("group", "tenant"), None),
        P(("group", "tenant")),
        P(("group", "tenant"), None),
        P("tenant", None, None),
        P("tenant", None, None),
        P(),
    )
    out_specs = (
        P(("group", "tenant"), None),
        P(("group", "tenant"), None, None),
        P(("group", "tenant"), None, None),
        P(("group", "tenant"), None),
    )
    return jax.shard_map(
        per_device, mesh=mesh, in_specs=in_specs, out_specs=out_specs, check_vma=False
    )
```

```python
import jax
import jax.numpy as jnp
import functools

from jax import lax
from jax.experimental import pallas as pl
from jax.experimental.pallas import tpu as pltpu
from jax.sharding import PartitionSpec as P

EXP_TEN = 8


adapter_scale_factor = 2.0


def routed(tokens, grad_up, tenant_ids, expert_ids, adapter_down, adapter_up, router):
    tok_rows = tokens.shape[0]
    model_width = tokens.shape[1]
    hidden_width = grad_up.shape[1]
    devices = lax.axis_size("tenant")
    capacity = 2 * tok_rows // devices
    buffer_len = devices * capacity
    global_ids = tenant_ids[:, None] * EXP_TEN + expert_ids
    logits = lax.dot_general(
        tokens, router, (((1,), (1,)), ((), ())), preferred_element_type=jnp.float32
    )
    picked = jnp.take_along_axis(logits, global_ids, axis=1)
    first_gate = jax.nn.sigmoid(picked[:, 0] - picked[:, 1])
    gate_sent = jnp.stack([first_gate, 1.0 - first_gate], axis=1).astype(jnp.bfloat16)
    flat_ids = global_ids.reshape(-1)
    slot_count = flat_ids.shape[0]
    same_owner = flat_ids[:, None] == flat_ids[None, :]
    slot_line = jnp.arange(slot_count, dtype=jnp.int32)
    earlier = slot_line[None, :] < slot_line[:, None]
    ranks = jnp.sum((same_owner & earlier).astype(jnp.int32), axis=1)
    places = (flat_ids * capacity + ranks).reshape(tok_rows, 2)

    def spread_rows(values):
        empty = jnp.zeros((buffer_len,) + values.shape[1:], values.dtype)
        return empty.at[places[:, 0]].set(values).at[places[:, 1]].set(values)

    send_rows = spread_rows(tokens).reshape(devices, capacity, model_width)
    send_grads = spread_rows(grad_up).reshape(devices, capacity, hidden_width)
    empty_gates = jnp.zeros((buffer_len,), jnp.bfloat16)
    send_gates = (
        empty_gates.at[places[:, 0]]
        .set(gate_sent[:, 0])
        .at[places[:, 1]]
        .set(gate_sent[:, 1])
        .reshape(devices, capacity)
    )
    recv_rows, recv_grads, recv_gates = (
        lax.all_to_all(send_rows, "tenant", split_axis=0, concat_axis=0, tiled=True),
        lax.all_to_all(send_grads, "tenant", split_axis=0, concat_axis=0, tiled=True),
        lax.all_to_all(send_gates, "tenant", split_axis=0, concat_axis=0, tiled=True),
    )
    rows_in = recv_rows.reshape(buffer_len, model_width)
    grads_in = recv_grads.reshape(buffer_len, hidden_width)
    incoming_gate_values = recv_gates.reshape(buffer_len).astype(jnp.float32)
    down = adapter_down[0]
    upper = adapter_up[0]
    reduced_rank_activations = lax.dot_general(
        rows_in, down, (((1,), (1,)), ((), ())), preferred_element_type=jnp.float32
    )
    returned_rank_gradient = lax.dot_general(
        grads_in, upper, (((1,), (1,)), ((), ())), preferred_element_type=jnp.float32
    )
    position_gate_value = (
        adapter_scale_factor * jnp.sum(reduced_rank_activations * returned_rank_gradient, axis=1)
    ).astype(jnp.bfloat16)
    gate_weighted_output = (
        adapter_scale_factor * incoming_gate_values[:, None] * returned_rank_gradient
    ).astype(jnp.bfloat16)
    scaled_reduced_activations = (
        adapter_scale_factor * incoming_gate_values[:, None] * reduced_rank_activations
    ).astype(jnp.bfloat16)
    slot_rows = jnp.dot(gate_weighted_output, down, preferred_element_type=jnp.float32).astype(
        jnp.bfloat16
    )
    back_rows, back_gates = (
        lax.all_to_all(
            slot_rows.reshape(devices, capacity, model_width),
            "tenant",
            split_axis=0,
            concat_axis=0,
            tiled=True,
        ),
        lax.all_to_all(
            position_gate_value.reshape(devices, capacity),
            "tenant",
            split_axis=0,
            concat_axis=0,
            tiled=True,
        ),
    )
    grad_down = lax.dot_general(
        gate_weighted_output, rows_in, (((0,), (0,)), ((), ())), preferred_element_type=jnp.float32
    )
    grad_upper = lax.dot_general(
        scaled_reduced_activations,
        grads_in,
        (((0,), (0,)), ((), ())),
        preferred_element_type=jnp.float32,
    )
    flat_back = back_rows.reshape(buffer_len, model_width)
    expert_grad = flat_back[places[:, 0]].astype(jnp.float32) + flat_back[places[:, 1]].astype(
        jnp.float32
    )
    gate_grads = back_gates.reshape(buffer_len)[places].astype(jnp.float32)
    logit_grad = first_gate * (1.0 - first_gate) * (gate_grads[:, 0] - gate_grads[:, 1])
    logit_sent = logit_grad.astype(jnp.bfloat16)
    columns = jnp.arange(router.shape[0], dtype=jnp.int32)[None, :]
    nothing = jnp.zeros((), jnp.bfloat16)
    signed = jnp.where(columns == global_ids[:, 0:1], logit_sent[:, None], nothing) - jnp.where(
        columns == global_ids[:, 1:2], logit_sent[:, None], nothing
    )
    router_term = jnp.dot(signed, router, preferred_element_type=jnp.float32)
    token_grad = (expert_grad + router_term).astype(jnp.bfloat16)
    router_grad = lax.psum_scatter(
        lax.dot_general(
            signed, tokens, (((0,), (0,)), ((), ())), preferred_element_type=jnp.float32
        ),
        "tenant",
        scatter_dimension=0,
        tiled=True,
    )
    return (token_grad, grad_down[None], grad_upper[None], router_grad)


F32 = jnp.float32
BF16 = jnp.bfloat16
TILE = 1024
PIECE = 512


def loop(count, body):
    def step(i, carry):
        body(i)
        return carry

    lax.fori_loop(0, count, step, 0)


def fused_kernel(
    tok_in, gup_in, ids, adn, aup, router,
    tok_out, dn_out, up_out, rt_out,
    tok, gup, fac, part, core_in, x_in, left_in, right_in,
    low, back, logits, wide, wide_t, scaled_t, sign_t, signed, acc,
    own_sem, ag_send, ag_recv, y_send, y_recv, core_send, core_recv, x_send, x_recv, z_send, left_recv, right_recv,
):
    me = lax.axis_index("tenant")
    g = lax.axis_index("group")
    c = lax.rem(me, 2)
    x = lax.rem(lax.div(me, 2), 2)
    z = lax.div(me, 4)
    model = tok.shape[1]
    hidden = gup.shape[1]
    half = hidden // 2
    both = model + hidden
    total = part.shape[2]
    rows = tok.shape[0]

    right = me + 4
    left = me - 4
    x_peer = me + 2 - 4 * x
    c_peer = me + 1 - 2 * c

    def slot(cc, zz, xx):
        return cc * 8 + zz * 2 + xx

    barrier = pltpu.get_barrier_semaphore()

    def greet(peer, group=g):
        pl.semaphore_signal(
            barrier,
            inc=1,
            device_id={"group": group, "tenant": peer},
            device_id_type=pl.DeviceIdType.MESH,
        )

    own = slot(c, z, x)
    own_dn = pltpu.make_async_copy(adn, fac.at[own, :, pl.ds(half, model)], own_sem.at[0])
    own_lo = pltpu.make_async_copy(
        aup.at[:, pl.ds(0, half)], fac.at[own, :, pl.ds(0, half)], own_sem.at[1]
    )
    own_hi = pltpu.make_async_copy(
        aup.at[:, pl.ds(half, half)], fac.at[own, :, pl.ds(half + model, half)], own_sem.at[2]
    )
    own_dn.start()
    own_lo.start()
    own_hi.start()
    load_tok = pltpu.make_async_copy(tok_in, tok, own_sem.at[3])
    load_gup = pltpu.make_async_copy(gup_in, gup, own_sem.at[4])
    load_tok.start()
    load_gup.start()
    greet(x_peer)
    greet(c_peer)
    greet(me, 1 - g)
    pl.when(z < 3)(lambda: greet(right))
    pl.when(z > 0)(lambda: greet(left))
    pl.semaphore_wait(
        barrier, 3 + jnp.where(z < 3, 1, 0).astype(jnp.int32) + jnp.where(z > 0, 1, 0).astype(jnp.int32)
    )
    own_dn.wait()
    own_lo.wait()
    own_hi.wait()

    def remote(src, dst, send, recv, peer, group=g):
        return pltpu.make_async_remote_copy(
            src_ref=src, dst_ref=dst, send_sem=send, recv_sem=recv,
            device_id={"group": group, "tenant": peer}, device_id_type=pl.DeviceIdType.MESH,
        )

    gathered = pl.ds(pl.multiple_of(g * half, 128), half + model)
    mine_y = pl.ds(pl.multiple_of(g * (half + model), 128), half)
    other_y = pl.ds(pl.multiple_of((1 - g) * (half + model), 128), half)

    def gather_copy(at, send_at, peer):
        block = fac.at[at, :, gathered]
        return remote(block, block, ag_send.at[send_at], ag_recv.at[at], peer)

    def to_y(zz, xx):
        at = slot(c, zz, xx)
        block = fac.at[at, :, mine_y]
        return remote(block, block, y_send.at[zz * 2 + xx], y_recv.at[at], me, 1 - g)

    def y_to_core(zz, xx):
        at = slot(c, zz, xx)
        block = fac.at[at, :, other_y]
        return remote(block, block, y_send.at[8 + zz * 2 + xx], y_recv.at[at], c_peer)

    def y_arrived(at):
        block = fac.at[at, :, other_y]
        remote(block, block, y_send.at[0], y_recv.at[at], c_peer).wait_recv()

    def to_right(zz):
        return gather_copy(slot(c, zz, x), zz, right)

    def to_left(zz):
        return gather_copy(slot(c, zz, x), 4 + zz, left)

    def to_x(zz):
        return gather_copy(slot(c, zz, x), 8 + zz, x_peer)

    def to_core(zz, xx):
        return gather_copy(slot(c, zz, xx), 12 + zz * 2 + xx, c_peer)

    def arrived(at):
        gather_copy(at, 0, c_peer).wait_recv()

    pl.when(z < 3)(lambda: to_right(z).start())
    pl.when(z > 0)(lambda: to_left(z).start())
    to_x(z).start()
    to_core(z, x).start()
    y_to_core(z, x).start()

    nt = (((1,), (1,)), ((), ()))
    logits[...] = jnp.zeros_like(logits)

    def logit_tile(i):
        cols = pl.ds(pl.multiple_of(i * TILE, TILE), TILE)
        logits[...] += lax.dot_general(tok[:, cols], router[:, cols], nt, preferred_element_type=F32)

    load_tok.wait()
    loop(model // TILE, logit_tile)

    for s in range(1, 4):
        def from_left(s=s):
            arrived(slot(c, z - s, x))
            pl.when(z < 3)(lambda: to_right(z - s).start())
            to_x(z - s).start()
            to_y(z - s, x).start()
            to_core(z - s, x).start()

        def from_right(s=s):
            arrived(slot(c, z + s, x))
            pl.when(z > 0)(lambda: to_left(z + s).start())
            to_x(z + s).start()
            to_y(z + s, x).start()
            to_core(z + s, x).start()

        pl.when(z - s >= 0)(from_left)
        pl.when(z + s <= 3)(from_right)

    def x_block(zz):
        arrived(slot(c, zz, 1 - x))
        to_y(zz, 1 - x).start()
        to_core(zz, 1 - x).start()

    def y_block(zz, xx):
        y_arrived(slot(c, zz, xx))
        y_to_core(zz, xx).start()

    x_block(z)
    for s in range(1, 4):
        for inside, zz in ((z - s >= 0, z - s), (z + s <= 3, z + s)):
            pl.when(inside)(functools.partial(y_block, zz, x))
            pl.when(inside)(functools.partial(x_block, zz))
    y_block(z, 1 - x)
    for s in range(1, 4):
        for inside, zz in ((z - s >= 0, z - s), (z + s <= 3, z + s)):
            pl.when(inside)(functools.partial(y_block, zz, 1 - x))
    for k in range(8):
        arrived((1 - c) * 8 + k)

    def factor_tile(start):
        return fac[:, :, pl.ds(start, TILE)].reshape(256, TILE)

    low[...] = jnp.zeros_like(low)
    back[...] = jnp.zeros_like(back)

    def low_tile(i):
        start = pl.multiple_of(i * TILE, TILE)
        low[...] += lax.dot_general(
            tok[:, pl.ds(start, TILE)],
            factor_tile(pl.multiple_of(half + start, TILE)),
            nt,
            preferred_element_type=F32
        )

    def back_tile(i):
        start = pl.multiple_of(i * TILE, TILE)
        back[...] += lax.dot_general(
            gup[:, pl.ds(start, TILE)],
            factor_tile(pl.multiple_of(start + jnp.where(start >= half, model, 0), TILE)),
            nt,
            preferred_element_type=F32,
        )

    loop(model // TILE, low_tile)
    load_gup.wait()
    per_half = half // TILE
    loop(per_half, lambda i: back_tile(i + g * per_half))
    for k in range(8):
        y_arrived((1 - c) * 8 + k)
    loop(per_half, lambda i: back_tile(i + (1 - g) * per_half))

    first = ids[:, 0:1]
    second = ids[:, 1:2]
    narrow = lax.broadcasted_iota(jnp.int32, (rows, 16), 1)
    n_sign = jnp.where(narrow == first, 1.0, 0.0) - jnp.where(narrow == second, 1.0, 0.0)
    first_gate = jax.nn.sigmoid(jnp.sum(logits[...] * n_sign, axis=1, keepdims=True))
    place = lax.broadcasted_iota(jnp.int32, (rows, 256), 1) // 16
    expert = (place % 8) * 2 + place // 8
    hot1 = expert == first
    hot2 = expert == second
    one = first_gate.astype(BF16).astype(F32)
    two = (1.0 - first_gate).astype(BF16).astype(F32)
    gates = adapter_scale_factor * (jnp.where(hot1, one, 0.0) + jnp.where(hot2, two, 0.0))
    lows = low[...]
    backs = back[...]
    weighted = gates * backs
    product = lows * backs

    def slot_gate(hot):
        picked = jnp.sum(jnp.where(hot, product, 0.0), axis=1, keepdims=True)
        return (adapter_scale_factor * picked).astype(BF16).astype(F32)

    logit_sent = first_gate * (1.0 - first_gate) * (slot_gate(hot1) - slot_gate(hot2))
    signed[...] = (logit_sent * n_sign).astype(BF16)
    w_sign = jnp.where(hot1, logit_sent, 0.0) - jnp.where(hot2, logit_sent, 0.0)
    wide[...] = weighted.astype(BF16)
    wide_t[...] = weighted.T.astype(BF16)
    scaled_t[...] = (gates * lows).T.astype(BF16)
    sign_t[...] = w_sign.T.astype(BF16)

    chunks = ((0, model), (model, half), (model + half, half + PIECE))

    def dn_products():
        def tile(i):
            cols = pl.ds(pl.multiple_of(i * PIECE, PIECE), PIECE)
            made = jnp.dot(wide_t[...], tok[:, cols], preferred_element_type=F32)
            part[:, :, cols] = made.astype(BF16).reshape(16, 16, PIECE)

        loop(model // PIECE, tile)

    def up_products(start):
        def tile(i):
            at = pl.multiple_of(start + i * PIECE, PIECE)
            made = jnp.dot(scaled_t[...], gup[:, pl.ds(at, PIECE)], preferred_element_type=F32)
            part[:, :, pl.ds(pl.multiple_of(model + at, PIECE), PIECE)] = made.astype(BF16).reshape(
                16, 16, PIECE
            )

        loop(half // PIECE, tile)

    def router_products():
        acc[...] = jnp.zeros_like(acc)
        line = lax.broadcasted_iota(jnp.int32, (256, PIECE), 0) % 16

        def tile(i):
            cols = pl.ds(pl.multiple_of(i * PIECE, PIECE), PIECE)
            made = jnp.dot(sign_t[...], tok[:, cols], preferred_element_type=F32)
            acc[...] = jnp.where(line == i, made, acc[...])

        loop(16, tile)
        part[:, :, pl.ds(both, PIECE)] = acc[...].astype(BF16).reshape(16, 16, PIECE)

    def order(k):
        low_half = (3, 2, 1 - z, z)[k]
        high_half = (0, 1, 5 - z, z)[k]
        return jnp.where(z < 2, low_half, high_half)

    def reduce_copy(q, source, target, to, send, recv, sem_at, peer):
        cols = pl.ds(*chunks[q])
        return remote(
            part.at[source, :, cols], target.at[to, :, cols],
            send.at[q, sem_at], recv.at[q, sem_at], peer,
        )

    def core_copy(q, zz, xx):
        at = zz * 2 + xx
        return reduce_copy(
            q, slot(1 - c, zz, xx), core_in, at, core_send, core_recv, at, c_peer
        )

    def x_copy(q, zz):
        return reduce_copy(q, slot(c, zz, 1 - x), x_in, zz, x_send, x_recv, zz, x_peer)

    def right_copy(q, zz):
        return reduce_copy(q, slot(c, zz, x), left_in, zz, z_send, left_recv, zz, right)

    def left_copy(q, zz):
        return reduce_copy(q, slot(c, zz, x), right_in, zz, z_send, right_recv, zz, left)

    def add(q, at, buf, index):
        begin, size = chunks[q]

        def add_cols(cols):
            part[at, :, cols] = (
                part[at, :, cols].astype(F32) + buf[index, :, cols].astype(F32)
            ).astype(BF16)

        loop(size // 2048, lambda i: add_cols(pl.ds(pl.multiple_of(begin + i * 2048, PIECE), 2048)))
        if size % 2048:
            add_cols(pl.ds(begin + size // 2048 * 2048, size % 2048))

    def to_core_peer(q):
        for k in range(4):
            core_copy(q, order(k), 1 - x).start()
        for k in range(4):
            core_copy(q, order(k), x).start()

    def x_stage(q):
        for k in range(4):
            d = order(k)
            core_copy(q, d, 1 - x).wait_recv()
            add(q, slot(c, d, 1 - x), core_in, d * 2 + 1 - x)
            x_copy(q, d).start()

    def own_stage(q):
        for k in range(4):
            d = order(k)
            core_copy(q, d, x).wait_recv()
            add(q, slot(c, d, x), core_in, d * 2 + x)

    dn_products()
    to_core_peer(0)
    up_products(0)
    to_core_peer(1)
    x_stage(0)
    up_products(half)
    router_products()
    to_core_peer(2)
    x_stage(1)
    own_stage(0)
    x_stage(2)

    def token_tile(i):
        start = pl.multiple_of(i * TILE, TILE)
        cols = pl.ds(start, TILE)
        tok_out[:, cols] = (
            jnp.dot(
                wide[...], factor_tile(pl.multiple_of(half + start, TILE)), preferred_element_type=F32
            )
            + jnp.dot(signed[...], router[:, cols], preferred_element_type=F32)
        ).astype(BF16)

    def z_stage(q):
        for k in range(3):
            d = order(k)
            mine = slot(c, d, x)
            x_copy(q, d).wait_recv()
            add(q, mine, x_in, d)

            def rightward(d=d, mine=mine):
                def more():
                    right_copy(q, d).wait_recv()
                    add(q, mine, left_in, d)

                pl.when(z > 0)(more)
                right_copy(q, d).start()

            def leftward(d=d, mine=mine):
                def more():
                    left_copy(q, d).wait_recv()
                    add(q, mine, right_in, d)

                pl.when(z < 3)(more)
                left_copy(q, d).start()

            pl.when(d > z)(rightward)
            pl.when(d < z)(leftward)

    z_stage(0)
    own_stage(1)
    z_stage(1)
    own_stage(2)
    loop(model // TILE, token_tile)
    z_stage(2)

    def results(body):
        def dn_tile(i):
            start = pl.multiple_of(i * TILE, TILE)
            body(dn_out, pl.ds(start, TILE), pl.ds(start, TILE))

        def up_tile(i):
            start = pl.multiple_of(i * TILE, TILE)
            body(up_out, pl.ds(start, TILE), pl.ds(pl.multiple_of(model + start, TILE), TILE))

        loop(model // TILE, dn_tile)
        loop(hidden // TILE, up_tile)
        body(rt_out, pl.ds(0, PIECE), pl.ds(both, PIECE))

    def first_terms(out, here, there):
        out[:, here] = part[own, :, there].astype(F32) + x_in[z, :, there].astype(F32)

    def left_term(out, here, there):
        out[:, here] += left_in[z, :, there].astype(F32)

    def right_term(out, here, there):
        out[:, here] += right_in[z, :, there].astype(F32)

    def take_left():
        for q in range(3):
            right_copy(q, z).wait_recv()
        results(left_term)

    def take_right():
        for q in range(3):
            left_copy(q, z).wait_recv()
        results(right_term)

    for q in range(3):
        x_copy(q, z).wait_recv()
    results(first_terms)
    pl.when(z > 0)(take_left)
    pl.when(z < 3)(take_right)

    for zz in range(4):
        pl.when((z < 3) & (zz <= z))(lambda zz=zz: to_right(zz).wait_send())
        pl.when((z > 0) & (zz >= z))(lambda zz=zz: to_left(zz).wait_send())
        to_x(zz).wait_send()
        for q in range(3):
            x_copy(q, zz).wait_send()
            pl.when(zz > z)(lambda q=q, zz=zz: right_copy(q, zz).wait_send())
            pl.when(zz < z)(lambda q=q, zz=zz: left_copy(q, zz).wait_send())
        for xx in range(2):
            to_core(zz, xx).wait_send()
            y_to_core(zz, xx).wait_send()
            pl.when((zz != z) | (xx != x))(lambda zz=zz, xx=xx: to_y(zz, xx).wait_send())
            for q in range(3):
                core_copy(q, zz, xx).wait_send()


def fused(tokens, grad_up, tenant_ids, expert_ids, adapter_down, adapter_up, router):
    rows, model = tokens.shape
    hidden = grad_up.shape[1]
    rank = adapter_down.shape[1]
    both = model + hidden
    total = both + PIECE
    ids = tenant_ids[:, None] * EXP_TEN + expert_ids
    vmem = pl.BlockSpec(memory_space=pltpu.VMEM)
    hbm = pl.BlockSpec(memory_space=pl.ANY)
    dma = pltpu.SemaphoreType.DMA
    tok_out, dn_out, up_out, rt_out = pl.pallas_call(
        fused_kernel,
        out_shape=(
            jax.ShapeDtypeStruct((rows, model), BF16),
            jax.ShapeDtypeStruct((rank, model), F32),
            jax.ShapeDtypeStruct((rank, hidden), F32),
            jax.ShapeDtypeStruct((16, PIECE), F32),
        ),
        in_specs=[hbm, hbm, vmem, hbm, hbm, vmem],
        out_specs=(vmem,) * 4,
        scratch_shapes=[
            pltpu.VMEM((rows, model), BF16),
            pltpu.VMEM((rows, hidden), BF16),
            pltpu.VMEM((16, rank, both), BF16),
            pltpu.VMEM((16, rank, total), BF16),
            pltpu.VMEM((8, rank, total), BF16),
            pltpu.VMEM((4, rank, total), BF16),
            pltpu.VMEM((4, rank, total), BF16),
            pltpu.VMEM((4, rank, total), BF16),
            pltpu.VMEM((rows, 256), F32),
            pltpu.VMEM((rows, 256), F32),
            pltpu.VMEM((rows, 16), F32),
            pltpu.VMEM((rows, 256), BF16),
            pltpu.VMEM((256, rows), BF16),
            pltpu.VMEM((256, rows), BF16),
            pltpu.VMEM((256, rows), BF16),
            pltpu.VMEM((rows, 16), BF16),
            pltpu.VMEM((256, PIECE), F32),
            dma((5,)), dma((20,)), dma((16,)), dma((16,)), dma((16,)), dma((3, 8)), dma((3, 8)),
            dma((3, 4)), dma((3, 4)), dma((3, 4)), dma((3, 4)), dma((3, 4)),
        ],
        compiler_params=pltpu.CompilerParams(
            collective_id=0, has_side_effects=True, vmem_limit_bytes=60 * 1024 * 1024
        ),
    )(tokens, grad_up, ids, adapter_down[0], adapter_up[0], router)
    return (tok_out, dn_out[None], up_out[None], rt_out.reshape(1, model))


def per_device(tokens, grad_up, tenant_ids, expert_ids, adapter_down, adapter_up, router):
    planes = lax.axis_size("tenant") == 16 and lax.axis_size("group") == 2
    fits = planes and tokens.shape[0] == 128 and adapter_down.shape[1] == 16
    plan = fused if fits else routed
    return plan(tokens, grad_up, tenant_ids, expert_ids, adapter_down, adapter_up, router)


def solution(mesh):
    in_specs = (
        P(("group", "tenant"), None),
        P(("group", "tenant"), None),
        P(("group", "tenant")),
        P(("group", "tenant"), None),
        P("tenant", None, None),
        P("tenant", None, None),
        P(),
    )
    out_specs = (
        P(("group", "tenant"), None),
        P(("group", "tenant"), None, None),
        P(("group", "tenant"), None, None),
        P(("group", "tenant"), None),
    )
    return jax.shard_map(
        per_device, mesh=mesh, in_specs=in_specs, out_specs=out_specs, check_vma=False
    )
```
